32 devices in a mesh: groups: 2 (over y), lat: 8 (over z, x), seq: 2 (over core).
Axes of the slice: x: 2, y: 2, z: 4, core: 2. Of those that a mesh axis runs over, the one named last changes fastest.
Arguments:
- residual: bfloat16 [1024, 3584], P(('groups', 'lat', 'seq')), parts along dimension 0, may hold values from -6 to 6
- gradient: bfloat16 [1024, 3584], P(('groups', 'lat', 'seq')), parts along dimension 0, may hold values from -6 to 6
- block_ids: int32 [1024, 4], P(('groups', 'lat', 'seq')), parts along dimension 0, may hold values from 0 to 7, all different within a row; in each aligned block of 32 rows (0 to 31, 32 to 63, ...) at most 24 rows name the same one
- jump_mask: int32 [1024, 4, 128], P(('groups', 'lat', 'seq')), parts along dimension 0, may hold values 0 or 1
- encoder: bfloat16 [3584, 1024], P(None, 'lat'), may hold values from -0.09375 to 0.09375
- enc_bias: float32 [1024], P('lat'), may hold values from -6 to 6
- decoder: bfloat16 [1024, 3584], P('lat'), may hold values from -0.25 to 0.25
- dec_bias: float32 [3584], replicated, may hold values from -6 to 6
Outputs:
- latent_codes: bfloat16 [1024, 4, 128], P(('groups', 'lat', 'seq')), parts along dimension 0
- attribution: float32 [1024, 4, 128], P(('groups', 'lat', 'seq')), parts along dimension 0
- recon_error: bfloat16 [1024, 3584], P(('groups', 'lat', 'seq')), parts along dimension 0
- latent_totals: float32 [2048], P(('groups', 'lat', 'seq')), parts along dimension 0
The draws below stay inside these ranges and needn't reach their ends.
There are 2 independent parts, one for each index of `groups`. The reference program is written for one: setup_inputs(seed, part) draws one part's arguments, and reference() takes and returns one part's arrays. A program takes and returns all parts, laid end to end along the dimension named above; an argument that names none is the same for every part. Nothing has to cross between parts.
Inputs may be any that keep to these rules, and one draw needn't show every extreme that they name: `block_ids`: each token names 4 different blocks. Among the rows of one device no block is named more than 24 times, and in every draw some device's rows name one block exactly 24 times.
All inputs are finite; a program needn't handle non-finite values. No bound on the sum of `jump_mask` on one device may be relied on, other than what follows from the above.
Results may differ from the reference program's by a relative error of at most 0.0044.
Values may be sent and summed in bfloat16 or wider, within the bound.
No kernel may reach another device: no remote copies, remote signals or barrier semaphores. Data moves between devices by JAX's collectives and lax.ppermute only.
A program may use at most 64 MiB of HBM per device.

```python
import math
import jax
import jax.numpy as jnp
import numpy as np
from jax import lax

D = 3584
BLK = 128
K = 4
TOK_DEV = 32
NBLK = 8
LATENTS = 1024
TOKENS = 512
CAP = 24
N_LAT = 8
N_SEQ = 2


def with_ends(entries, stream_key, low, high):
    longest = entries.shape.index(max(entries.shape))
    spots = []
    for shift in (0, 1):
        where = [jax.random.randint(jax.random.fold_in(stream_key, axis), (), 0, length) for axis, length in enumerate(entries.shape)]
        where[longest] = (where[longest] + shift) % entries.shape[longest]
        spots.append(tuple(where))
    return entries.at[spots[0]].set(low).at[spots[1]].set(high)


def block_levels(own_key, extent, shards, smallest, largest):
    loudness, own = 1.0, jax.random.fold_in(own_key, 6)
    for dim, shards_of in shards:
        heights = jnp.exp(jax.random.uniform(jax.random.fold_in(own, dim), (shards_of,), jnp.float32, smallest / len(shards), largest / len(shards)))
        loudness = loudness * jnp.repeat(heights, extent[dim] // shards_of).reshape([-1 if axis == dim else 1 for axis in range(len(extent))])
    return loudness


def assign_block(stream_key, own, number, rows, count, top, limit, lean):
    ranking = jax.random.permutation(stream_key, count)
    crowded, ordinary = shares(count, rows * top, limit, lean, True), shares(count, rows * top, limit, lean, False)
    places = jnp.arange(count)

    def named(tallies, turn):
        used = int((tallies > 0).sum())
        fixed = max(1, used // 4)
        moved = fixed + (places - fixed + turn * (used - fixed)) % max(1, count - fixed)
        return jnp.zeros((count,), jnp.int32).at[ranking[jnp.where(places < fixed, places, moved)]].set(jnp.asarray(tallies, jnp.int32))

    tallies = jnp.where(number % 4 == 0, named(crowded, number // 4), named(ordinary, number - number // 4 - 1))
    mixed = jax.random.permutation(jax.random.fold_in(own, 3), count)
    source_of, sink = mixed[0:count // 2 * 2:2], mixed[1:count // 2 * 2:2]
    room = jnp.minimum(tallies[source_of] - 1, limit - tallies[sink]) // 2
    room = jnp.where((source_of == ranking[0]) | (sink == ranking[0]) | (tallies[sink] == 0), 0, jnp.maximum(room, 0))
    moved = jax.random.randint(jax.random.fold_in(own, 4), (count // 2,), 0, 1 << 20) % (room + 1)
    tallies = tallies.at[source_of].add(-moved).at[sink].add(moved)
    labels = jnp.searchsorted(jnp.cumsum(tallies), jnp.arange(rows * top), side="right").astype(jnp.int32)
    listing = labels.reshape(top, rows).T
    listing = listing[jax.random.permutation(jax.random.fold_in(own, 1), rows)]
    turn = jax.random.randint(jax.random.fold_in(own, 2), (rows, 1), 0, top)
    return jnp.take_along_axis(listing, (jnp.arange(top)[None, :] + turn) % top, axis=1)


def shares(number_of, total, limit, skew, full):
    weights = [(1 << 20) // math.isqrt(grade ** skew) + 1 for grade in range(1, number_of + 1)]
    largest = limit if full else min(limit, max(-(-total // number_of), total * weights[0] // sum(weights)))
    least = 1 if total - largest >= number_of - 1 else 0
    given, surplus = [largest] + [least] * (number_of - 1), total - largest - least * (number_of - 1)
    while surplus > 0:
        candidates = [i for i in range(1, number_of) if given[i] < largest] or [i for i in range(1, number_of) if given[i] < limit]
        mass, remaining = sum([weights[i] for i in candidates]), surplus
        for i in candidates:
            addition = min(limit - given[i], max(1, remaining * weights[i] // mass), surplus)
            given[i] = given[i] + addition
            surplus = surplus - addition
    return np.array(given)


def scatter_about(rng, shape, spread, bound, split=(), held_as=jnp.bfloat16):
    entries = jax.random.normal(rng, shape, jnp.float32) * spread
    if len(split) > 0:
        entries = block_levels(rng, shape, split, -0.22, 0.18) * entries
    return jnp.clip(entries, min=-bound, max=bound).astype(held_as)


def setup_inputs(seed: int = 0, part: int = 0) -> dict:
    key_of = jax.random.split(jax.random.key(seed), 9)
    part_keys = jax.random.split(jax.random.fold_in(key_of[8], part), 9)
    residual = scatter_about(part_keys[0], (TOKENS, D), 1.0, 6.0, ((0, 16),))
    gradient = scatter_about(part_keys[1], (TOKENS, D), 1.0, 6.0, ((0, 16),))
    block_ids_keys = jax.random.split(jax.random.fold_in(part_keys[2], 1), TOKENS // TOK_DEV)
    block_ids_turns = jax.random.permutation(jax.random.fold_in(part_keys[2], 3), TOKENS // TOK_DEV)
    block_ids = jax.vmap(lambda own, number: assign_block(jax.random.fold_in(part_keys[2], 2), own, number, TOK_DEV, NBLK, K, CAP, 2))(block_ids_keys, block_ids_turns).reshape((TOKENS, K))
    jump_mask = with_ends((jax.random.randint(part_keys[3], (TOKENS, K, BLK), 0, 2) < 1).astype(jnp.int32), jax.random.fold_in(part_keys[3], 1), 0, 1)
    encoder = scatter_about(key_of[4], (D, LATENTS), D ** -0.5, 0.09375, ((1, 8),))
    enc_bias = scatter_about(key_of[5], (LATENTS,), 1.0, 6.0, ((0, 8),), jnp.float32)
    decoder = scatter_about(key_of[6], (LATENTS, D), (K * BLK) ** -0.5, 0.25, ((0, 8),))
    dec_bias = scatter_about(key_of[7], (D,), 1.0, 6.0, (), jnp.float32)
    return dict(residual=residual, gradient=gradient, block_ids=block_ids, jump_mask=jump_mask, encoder=encoder, enc_bias=enc_bias, decoder=decoder, dec_bias=dec_bias)


def reference(residual, gradient, block_ids, jump_mask, encoder, enc_bias, decoder, dec_bias):
    slot_count = TOKENS * K
    room = CAP * N_LAT * N_SEQ
    flat_blocks = block_ids.reshape(slot_count).astype(jnp.int32)
    sorted_slots = jnp.argsort(flat_blocks, stable=True).astype(jnp.int32)
    block_range = jnp.arange(NBLK, dtype=jnp.int32)
    counts = jnp.sum((flat_blocks[:, None] == block_range[None, :]).astype(jnp.int32), axis=0)
    starts = (jnp.cumsum(counts) - counts).astype(jnp.int32)
    mask_values = jump_mask.reshape(slot_count, BLK).astype(jnp.float32)

    def per_block(carry, which):
        codes_acc, score_acc, recon_acc = carry
        offsets = jnp.arange(room, dtype=jnp.int32)
        valid = (offsets < counts[which])[:, None]
        position = jnp.minimum(starts[which] + offsets, slot_count - 1).astype(jnp.int32)
        slots = sorted_slots[position]
        tokens = slots // K
        enc_cols = lax.dynamic_slice_in_dim(encoder, (which * BLK).astype(jnp.int32), BLK, 1)
        dec_rows = lax.dynamic_slice_in_dim(decoder, (which * BLK).astype(jnp.int32), BLK, 0)
        bias_part = lax.dynamic_slice_in_dim(enc_bias, (which * BLK).astype(jnp.int32), BLK, 0)
        preact = jnp.dot(residual[tokens], enc_cols, preferred_element_type=jnp.float32) + bias_part
        codes = (preact * mask_values[slots]).astype(jnp.bfloat16)
        projected = jnp.dot(gradient[tokens], dec_rows.T, preferred_element_type=jnp.float32)
        scores = codes.astype(jnp.float32) * projected
        recon = jnp.dot(codes, dec_rows, preferred_element_type=jnp.float32).astype(jnp.bfloat16)
        zero = jnp.zeros((), jnp.float32)
        codes_acc = codes_acc.at[slots].add(jnp.where(valid, codes.astype(jnp.float32), zero))
        score_acc = score_acc.at[slots].add(jnp.where(valid, scores, zero))
        recon_acc = recon_acc.at[tokens].add(jnp.where(valid, recon.astype(jnp.float32), zero))
        summed = jnp.sum(jnp.where(valid, scores, zero), axis=0)
        return (codes_acc, score_acc, recon_acc), summed

    start_carry = (jnp.zeros((slot_count, BLK), jnp.float32), jnp.zeros((slot_count, BLK), jnp.float32), jnp.zeros((TOKENS, D), jnp.float32))
    (codes_acc, score_acc, recon_acc), totals = lax.scan(per_block, start_carry, block_range)
    latent_codes = codes_acc.astype(jnp.bfloat16).reshape(TOKENS, K, BLK)
    attribution = score_acc.reshape(TOKENS, K, BLK)
    recon_error = (residual.astype(jnp.float32) - dec_bias - recon_acc).astype(jnp.bfloat16)
    factor = (TOKENS * K / NBLK) ** -0.5
    latent_totals = totals.reshape(LATENTS) * factor
    return latent_codes, attribution, recon_error, latent_totals
```

```python
import jax
import jax.numpy as jnp
from jax import lax
from jax.sharding import PartitionSpec as P

AXES = ("groups", "lat", "seq")


def place_rows(values, source, filled, leading):
    picked = jnp.where(filled[:, None], values[source], jnp.zeros((), values.dtype))
    return picked.reshape(leading + (values.shape[-1],))


def move_tokens(residual, gradient, block_ids, jump_mask, encoder, enc_bias, decoder, dec_bias):
    tok_rows, width = residual.shape
    active = block_ids.shape[1]
    lanes = jump_mask.shape[2]
    lat_count = lax.axis_size("lat")
    seq_count = lax.axis_size("seq")
    local_blocks = encoder.shape[1] // lanes
    block_count = local_blocks * lat_count
    capacity = max(
        2, min(tok_rows, (3 * tok_rows * active + 2 * block_count - 1) // (2 * block_count))
    )
    slot_count = tok_rows * active
    flat_blocks = block_ids.reshape(slot_count)
    one_hot = (flat_blocks[:, None] == jnp.arange(block_count, dtype=jnp.int32)[None, :]).astype(
        jnp.int32
    )
    earlier = jnp.sum(jnp.cumsum(one_hot, axis=0) * one_hot, axis=1) - 1
    slot_id = flat_blocks * capacity + earlier
    owner_row = (
        jnp.zeros((block_count * capacity,), jnp.int32)
        .at[slot_id]
        .set(jnp.arange(slot_count, dtype=jnp.int32) + 1)
    )
    filled = owner_row > 0
    slot_source = jnp.maximum(owner_row - 1, 0)
    token_source = slot_source // active
    leading = (lat_count, local_blocks, capacity)
    enc_blocks = encoder.reshape(width, local_blocks, lanes)
    dec_blocks = decoder.reshape(local_blocks, lanes, width)
    bias_blocks = enc_bias.reshape(1, local_blocks, 1, lanes)
    mask_values = jump_mask.astype(jnp.float32)
    total_tokens = tok_rows * lat_count * seq_count
    factor = (total_tokens * active / block_count) ** (-0.5)

    def gather_home(slotted):
        last = slotted.shape[-1]
        return slotted.reshape(block_count * capacity, last)[slot_id].reshape(
            tok_rows, active, last
        )

    def swap(values):
        return lax.all_to_all(values, "lat", split_axis=0, concat_axis=0, tiled=True)

    residual_slots = place_rows(residual, token_source, filled, leading)
    gradient_slots = place_rows(gradient, token_source, filled, leading)
    preact = jnp.einsum(
        "sbcd,dbj->sbcj", swap(residual_slots), enc_blocks, preferred_element_type=jnp.float32
    )
    preact = swap((preact + bias_blocks).astype(jnp.bfloat16)).astype(jnp.float32)
    latent_codes = (gather_home(preact) * mask_values).astype(jnp.bfloat16)
    code_slots = place_rows(latent_codes.reshape(slot_count, lanes), slot_source, filled, leading)
    code_data = swap(code_slots)
    grad_data = swap(gradient_slots)
    score_data = code_data.astype(jnp.float32) * jnp.einsum(
        "sbcd,bjd->sbcj", grad_data, dec_blocks, preferred_element_type=jnp.float32
    )
    recon_data = jnp.einsum(
        "sbcj,bjd->sbcd", code_data, dec_blocks, preferred_element_type=jnp.float32
    )
    recon_home = gather_home(swap(recon_data.astype(jnp.bfloat16)))
    attribution = gather_home(swap(score_data))
    recon_error = (
        residual.astype(jnp.float32) - dec_bias - jnp.sum(recon_home.astype(jnp.float32), axis=1)
    ).astype(jnp.bfloat16)
    term = jnp.dot(
        one_hot.T.astype(jnp.float32),
        attribution.reshape(slot_count, lanes),
        precision=lax.Precision.HIGHEST,
    )
    latent_totals = (
        lax.psum_scatter(
            term.reshape(block_count * lanes), ("lat", "seq"), scatter_dimension=0, tiled=True
        )
        * factor
    )
    return (latent_codes, attribution, recon_error, latent_totals)


def nt(a, b):
    return lax.dot_general(a, b, (((1,), (1,)), ((), ())), preferred_element_type=jnp.float32)


def move_weights(residual, gradient, block_ids, jump_mask, encoder, enc_bias, decoder, dec_bias):
    tok, width = residual.shape
    active = block_ids.shape[1]
    lanes = jump_mask.shape[2]
    lat_count = lax.axis_size("lat")
    ring = lat_count // 2
    per = lanes // 4
    half = width // 2
    bf = jnp.bfloat16
    f32 = jnp.float32
    g = lax.axis_index("groups")
    lat = lax.axis_index("lat")
    s = lax.axis_index("seq")
    z, x = lat // 2, lat % 2
    q = 2 * s + g

    def permute(values, to):
        pairs = []
        for gg in range(2):
            for ll in range(lat_count):
                for ss in range(2):
                    a, b, c = to(gg, ll, ss)
                    pairs.append(((gg * lat_count + ll) * 2 + ss, (a * lat_count + b) * 2 + c))
        return lax.ppermute(values, AXES, pairs)

    def by_x(v):
        return permute(v, lambda gg, ll, ss: (gg, ll ^ 1, ss))

    def by_y(v):
        return permute(v, lambda gg, ll, ss: (1 - gg, ll, ss))

    def by_core(v):
        return permute(v, lambda gg, ll, ss: (gg, ll, 1 - ss))

    def by_z(v, k):
        return permute(v, lambda gg, ll, ss: (gg, (ll + 2 * k) % lat_count, ss))

    lane_id = lax.broadcasted_iota(jnp.int32, (per, lanes), 1)
    row_id = lax.broadcasted_iota(jnp.int32, (per, lanes), 0)
    pick = (lane_id == row_id + per * q).astype(bf)
    enc_q = nt(pick, encoder).astype(bf)
    bias_q = lax.dynamic_slice_in_dim(enc_bias, q * per, per)
    hi = lax.reduce_precision(bias_q, 8, 7)
    mid = lax.reduce_precision(bias_q - hi, 8, 7)
    low = lax.reduce_precision(bias_q - hi - mid, 8, 7)
    bias_cols = jnp.stack([hi, mid, low], axis=1).astype(bf)
    enc_q = jnp.concatenate([enc_q, jnp.pad(bias_cols, ((0, 0), (0, 125)))], axis=1)
    dec_q = lax.dynamic_slice_in_dim(decoder, q * per, per)
    enc_parts, dec_parts = [enc_q], [dec_q]
    for _ in range(ring - 1):
        enc_parts.append(by_z(enc_parts[-1], 1))
        dec_parts.append(by_z(dec_parts[-1], 1))
    enc_all = jnp.concatenate(enc_parts, axis=0)
    dec_all = jnp.concatenate(dec_parts, axis=0)

    blocks = jnp.arange(lat_count, dtype=jnp.int32)
    named = block_ids[:, :, None] == blocks[None, None, :]
    mask = jnp.sum(
        jnp.where(named[:, :, :, None], jump_mask[:, :, None, :], 0), axis=1
    ).astype(bf).reshape(tok, lat_count * lanes)
    mh = lat_count * lanes // 2
    a0 = jnp.concatenate([residual[:, :half], gradient[:, :half], mask[:, :mh]], axis=1)
    b0 = jnp.concatenate([residual[:, half:], gradient[:, half:], mask[:, mh:]], axis=1)
    a1 = by_y(a0)
    b1 = by_x(b0)
    a01 = jnp.concatenate([a0, a1], axis=0)
    a2 = by_x(a01)
    b2 = by_y(jnp.concatenate([b0, b1], axis=0))
    mine = jnp.concatenate(
        [
            jnp.concatenate([a01, a2], axis=0),
            jnp.concatenate([b0, b2[:tok], b1, b2[tok:]], axis=0),
        ],
        axis=1,
    )
    rows = jnp.concatenate([mine, by_core(mine)], axis=0)
    side = 2 * half + mh
    res_a, res_b = rows[:, :half], rows[:, side : side + half]
    grad_a, grad_b = rows[:, half : 2 * half], rows[:, side + half : side + 2 * half]
    mask_all = jnp.concatenate([rows[:, 2 * half : side], rows[:, side + 2 * half :]], axis=1)
    n_rows = rows.shape[0]

    def source_lane(c, zz, xx, qq):
        return (((zz - c // per) % ring) * 2 + xx) * lanes + qq * per + c % per

    width_all = lat_count * lanes
    mine_lanes = ring * per
    want = source_lane(lax.broadcasted_iota(jnp.int32, (mine_lanes, width_all), 0), z, x, q)
    pick_mask = (want == lax.broadcasted_iota(jnp.int32, (mine_lanes, width_all), 1)).astype(bf)
    mask_here = nt(mask_all, pick_mask)

    preact = (
        nt(res_a, enc_all[:, :half])
        + nt(res_b, enc_all[:, half:width])
        + nt(jnp.ones((n_rows, 128), bf), enc_all[:, width:])
    )
    codes = (preact * mask_here).astype(bf)
    projected = nt(grad_a, dec_all[:, :half]) + nt(grad_b, dec_all[:, half:])
    scores = codes.astype(f32) * projected
    recon = jnp.dot(codes, dec_all, preferred_element_type=f32).astype(bf)
    scores_b = scores.astype(bf)

    by_kind = scores.reshape(2, 2, 2, tok, mine_lanes).sum(axis=(0, 1, 3))
    sums = by_kind[:, :per]
    for k in range(1, ring):
        sums = sums + by_z(by_kind, -k)[:, per * k : per * k + per]
    other = by_y(sums[1])
    factor = (tok * lat_count * 2 * active / lat_count) ** (-0.5)
    latent_totals = (
        jnp.where(g == 0, jnp.concatenate([sums[0], other]), jnp.concatenate([other, sums[0]]))
        * factor
    )

    hr = n_rows // 2
    keep = jnp.concatenate([recon, codes, scores_b], axis=1)
    got = by_core(keep[hr:])
    summed = recon[:hr].astype(f32) + got[:, :width].astype(f32)
    code_two = jnp.concatenate([codes[:hr], got[:, width : width + mine_lanes]], axis=1)
    score_two = jnp.concatenate([scores_b[:hr], got[:, width + mine_lanes :]], axis=1)
    sum_a, sum_b = summed[:, :half], summed[:, half:]
    pa = jnp.concatenate([sum_a.astype(bf), code_two], axis=1)
    pb = jnp.concatenate([sum_b.astype(bf), score_two], axis=1).reshape(2, 2, tok, -1)
    got_a = by_x(pa[2 * tok :])
    got_b = by_y(pb[:, 1])
    sum_a = sum_a[: 2 * tok] + got_a[:, :half].astype(f32)
    sum_b = sum_b.reshape(2, 2, tok, half)[:, 0] + got_b[:, :, :half].astype(f32)
    code_four = jnp.concatenate([code_two[: 2 * tok], got_a[:, half:]], axis=1)
    score_four = jnp.concatenate([pb[:, 0, :, half:], got_b[:, :, half:]], axis=2)
    got_a = by_y(jnp.concatenate([sum_a[tok:].astype(bf), code_four[tok:]], axis=1))
    got_b = by_x(jnp.concatenate([sum_b[1].astype(bf), score_four[1]], axis=1))
    recon_home = jnp.concatenate(
        [
            sum_a[:tok] + got_a[:, :half].astype(f32),
            sum_b[0] + got_b[:, :half].astype(f32),
        ],
        axis=1,
    )
    recon_error = (residual.astype(f32) - dec_bias - recon_home).astype(bf)

    code_src = jnp.concatenate([code_four[:tok], got_a[:, half:]], axis=1)
    score_src = jnp.concatenate([score_four[0], got_b[:, half:]], axis=1)
    lane = lax.broadcasted_iota(jnp.int32, (width_all, width_all), 0)
    part, inner = lane // mine_lanes, lane % mine_lanes
    out_lane = lax.broadcasted_iota(jnp.int32, (width_all, width_all), 1)

    def spread(first, second):
        xx = x ^ first
        yy = g ^ second
        qq = 2 * (s ^ (part % 2)) + yy
        return (source_lane(inner, z, xx, qq) == out_lane).astype(bf)

    code_dense = jnp.dot(
        code_src, spread((part // 2) % 2, part // 4), preferred_element_type=f32
    ).reshape(tok, 1, lat_count, lanes)
    score_dense = jnp.dot(
        score_src, spread(part // 4, (part // 2) % 2), preferred_element_type=f32
    ).reshape(tok, 1, lat_count, lanes)
    chosen = named[:, :, :, None]
    latent_codes = jnp.sum(jnp.where(chosen, code_dense, 0.0), axis=2).astype(bf)
    attribution = jnp.sum(jnp.where(chosen, score_dense, 0.0), axis=2)
    return (latent_codes, attribution, recon_error, latent_totals)


def solution(mesh):
    sizes = dict(mesh.shape)

    def on_device(residual, gradient, block_ids, jump_mask, encoder, enc_bias, decoder, dec_bias):
        lanes = jump_mask.shape[2]
        small = (
            sizes["groups"] == 2
            and sizes["seq"] == 2
            and sizes["lat"] in (2, 4, 8, 16)
            and encoder.shape[1] == lanes
            and lanes % 64 == 0
            and residual.shape[1] % 256 == 0
        )
        body = move_weights if small else move_tokens
        return body(
            residual, gradient, block_ids, jump_mask, encoder, enc_bias, decoder, dec_bias
        )

    rows = P(("groups", "lat", "seq"), None)
    cubes = P(("groups", "lat", "seq"), None, None)
    return jax.shard_map(
        on_device,
        mesh=mesh,
        in_specs=(rows, rows, rows, cubes, P(None, "lat"), P("lat"), P("lat", None), P()),
        out_specs=(cubes, cubes, rows, P(("groups", "lat", "seq"))),
        check_vma=False,
    )
```

```python
import functools

import jax
import jax.numpy as jnp
from jax import lax
from jax.experimental import pallas as pl
from jax.experimental.pallas import tpu as pltpu
from jax.sharding import PartitionSpec as P

AXES = ("groups", "lat", "seq")


def place_rows(values, source, filled, leading):
    picked = jnp.where(filled[:, None], values[source], jnp.zeros((), values.dtype))
    return picked.reshape(leading + (values.shape[-1],))


def move_tokens(residual, gradient, block_ids, jump_mask, encoder, enc_bias, decoder, dec_bias):
    tok_rows, width = residual.shape
    active = block_ids.shape[1]
    lanes = jump_mask.shape[2]
    lat_count = lax.axis_size("lat")
    seq_count = lax.axis_size("seq")
    local_blocks = encoder.shape[1] // lanes
    block_count = local_blocks * lat_count
    capacity = max(
        2, min(tok_rows, (3 * tok_rows * active + 2 * block_count - 1) // (2 * block_count))
    )
    slot_count = tok_rows * active
    flat_blocks = block_ids.reshape(slot_count)
    one_hot = (flat_blocks[:, None] == jnp.arange(block_count, dtype=jnp.int32)[None, :]).astype(
        jnp.int32
    )
    earlier = jnp.sum(jnp.cumsum(one_hot, axis=0) * one_hot, axis=1) - 1
    slot_id = flat_blocks * capacity + earlier
    owner_row = (
        jnp.zeros((block_count * capacity,), jnp.int32)
        .at[slot_id]
        .set(jnp.arange(slot_count, dtype=jnp.int32) + 1)
    )
    filled = owner_row > 0
    slot_source = jnp.maximum(owner_row - 1, 0)
    token_source = slot_source // active
    leading = (lat_count, local_blocks, capacity)
    enc_blocks = encoder.reshape(width, local_blocks, lanes)
    dec_blocks = decoder.reshape(local_blocks, lanes, width)
    bias_blocks = enc_bias.reshape(1, local_blocks, 1, lanes)
    mask_values = jump_mask.astype(jnp.float32)
    total_tokens = tok_rows * lat_count * seq_count
    factor = (total_tokens * active / block_count) ** (-0.5)

    def gather_home(slotted):
        last = slotted.shape[-1]
        return slotted.reshape(block_count * capacity, last)[slot_id].reshape(
            tok_rows, active, last
        )

    def swap(values):
        return lax.all_to_all(values, "lat", split_axis=0, concat_axis=0, tiled=True)

    residual_slots = place_rows(residual, token_source, filled, leading)
    gradient_slots = place_rows(gradient, token_source, filled, leading)
    preact = jnp.einsum(
        "sbcd,dbj->sbcj", swap(residual_slots), enc_blocks, preferred_element_type=jnp.float32
    )
    preact = swap((preact + bias_blocks).astype(jnp.bfloat16)).astype(jnp.float32)
    latent_codes = (gather_home(preact) * mask_values).astype(jnp.bfloat16)
    code_slots = place_rows(latent_codes.reshape(slot_count, lanes), slot_source, filled, leading)
    code_data = swap(code_slots)
    grad_data = swap(gradient_slots)
    score_data = code_data.astype(jnp.float32) * jnp.einsum(
        "sbcd,bjd->sbcj", grad_data, dec_blocks, preferred_element_type=jnp.float32
    )
    recon_data = jnp.einsum(
        "sbcj,bjd->sbcd", code_data, dec_blocks, preferred_element_type=jnp.float32
    )
    recon_home = gather_home(swap(recon_data.astype(jnp.bfloat16)))
    attribution = gather_home(swap(score_data))
    recon_error = (
        residual.astype(jnp.float32) - dec_bias - jnp.sum(recon_home.astype(jnp.float32), axis=1)
    ).astype(jnp.bfloat16)
    term = jnp.dot(
        one_hot.T.astype(jnp.float32),
        attribution.reshape(slot_count, lanes),
        precision=lax.Precision.HIGHEST,
    )
    latent_totals = (
        lax.psum_scatter(
            term.reshape(block_count * lanes), ("lat", "seq"), scatter_dimension=0, tiled=True
        )
        * factor
    )
    return (latent_codes, attribution, recon_error, latent_totals)


BF = jnp.bfloat16
F32 = jnp.float32


def nt(a, b):
    return lax.dot_general(a, b, (((1,), (1,)), ((), ())), preferred_element_type=F32)


def call(kernel, outs, *args, flops=0, size=1 << 20):
    whole = pl.BlockSpec(memory_space=pltpu.VMEM)
    smem = pl.BlockSpec(memory_space=pltpu.SMEM)
    return pl.pallas_call(
        kernel,
        in_specs=[smem] + [whole] * (len(args) - 1),
        out_specs=[whole] * len(outs),
        out_shape=[jax.ShapeDtypeStruct(*o) for o in outs],
        compiler_params=pltpu.CompilerParams(vmem_limit_bytes=48 << 20),
        cost_estimate=pl.CostEstimate(flops=flops, bytes_accessed=size, transcendentals=0),
    )(*args)


def weights_kernel(place, enc, dec, bias, enc_out, dec_out):
    per, lanes = enc_out.shape[0], enc.shape[1]
    half = dec_out.shape[1]
    row = lax.broadcasted_iota(jnp.int32, (per, lanes), 0)
    lane = lax.broadcasted_iota(jnp.int32, (per, lanes), 1)
    pick = (lane == row + per * place[1]).astype(BF)
    enc_out[:, :half] = nt(pick, enc[...]).astype(BF)
    b = bias[...]
    hi = b.astype(BF).astype(F32)
    mid = (b - hi).astype(BF).astype(F32)
    low = b - hi - mid
    term = lax.broadcasted_iota(jnp.int32, (lanes, lanes), 0)
    terms = jnp.where(term == 0, hi, jnp.where(term == 1, mid, jnp.where(term == 2, low, 0.0)))
    enc_out[:, half:] = nt(pick, terms.astype(BF)).astype(BF)
    dec_out[...] = dec[...]


def target_block(lane, m, place, x_rel, ring):
    turn = place[2] - 2 * m - (lane >= 64).astype(jnp.int32)
    turn = jnp.where(turn < 0, turn + ring, turn)
    return turn * 2 + (place[0] ^ x_rel)


def tokens_kernel(ring, place, res, grad, ids, jump, keep, send):
    tok, width = res.shape
    half = width // 2
    active = ids.shape[1]
    here = pl.multiple_of(place[3] * half, 128)
    there = pl.multiple_of((1 - place[3]) * half, 128)
    keep[:, :half] = res[:, pl.ds(here, half)]
    keep[:, half:width] = grad[:, pl.ds(here, half)]
    send[:, :half] = res[:, pl.ds(there, half)]
    send[:, half:width] = grad[:, pl.ds(there, half)]
    lane = lax.broadcasted_iota(jnp.int32, (tok, 128), 1)
    low = lane < 64
    plain = [jump[:, k, :] for k in range(active)]
    moved = [pltpu.roll(v, 64, 1) for v in plain]
    for dest in range(4):
        x_rel, y_rel = dest % 2, dest // 2
        first = (place[1] ^ y_rel) == 0
        for m in range(ring // 2):
            tgt = target_block(lane, m, place, x_rel, ring)
            total = jnp.zeros((tok, 128), jnp.int32)
            for k in range(active):
                value = jnp.where(low == first, plain[k], moved[k])
                total = total + jnp.where(ids[:, k : k + 1] == tgt, value, 0)
            at = width + (dest * (ring // 2) + m) * 128
            out = total.astype(F32).astype(BF)
            keep[:, at : at + 128] = out
            send[:, at : at + 128] = out


def rows_kernel(place, keep, got, *outs):
    tok = keep.shape[0]
    width = outs[0].shape[1]
    names = (keep.shape[1] - width) // 3
    width = width - names
    for dest, out in enumerate(outs):
        at = width + (dest + 1) * names
        for i, src in enumerate((keep, got)):
            out[i * tok : (i + 1) * tok, :width] = src[:, :width]
            out[i * tok : (i + 1) * tok, width:] = src[:, at : at + names]


def preact_kernel(ring, half, place, keep, got, from_x, from_y, from_d, *refs):
    parts, out = refs[:ring], refs[ring]
    tok = keep.shape[0]
    per = parts[0].shape[0]
    weights = jnp.concatenate([p[:, :half] for p in parts], axis=0)
    extra = jnp.concatenate([p[:, half:] for p in parts], axis=0)
    ones = jnp.where(place[3] == 0, 1.0, 0.0) * jnp.ones((8, 128), F32)
    bias = nt(ones.astype(BF), extra)[:1]
    at = 0
    for src in (keep, got, from_x, from_y, from_d):
        n = src.shape[0]
        out[at : at + n] = nt(src[:, :half], weights) + bias
        at += n


def codes_kernel(place, mine, other, keep, got, from_x, from_y, from_d, out):
    tok = keep.shape[0]
    names = out.shape[1]
    base = keep.shape[1] - 4 * names
    for chip, src in enumerate((None, from_x, from_y, from_d)):
        for i in range(2):
            at = (2 * chip + i) * tok
            swapped = (2 * chip + 1 - i) * tok
            if chip == 0:
                mask = (keep, got)[i][:, base : base + names]
            else:
                mask = src[i * tok : (i + 1) * tok, base:]
            total = mine[at : at + tok] + other[swapped : swapped + tok]
            out[at : at + tok] = (total * mask.astype(F32)).astype(BF)


def recon_kernel(ring, half, place, codes, keep, got, from_x, from_y, from_d, *refs):
    parts = refs[:ring]
    own_recon, own_proj, sums = refs[ring : ring + 3]
    sends = refs[ring + 3 :]
    tok = keep.shape[0]
    names = codes.shape[1]
    weights = jnp.concatenate([p[...] for p in parts], axis=0)
    totals = []
    for chip, src in enumerate((None, from_x, from_y, from_d)):
        at = chip * 2 * tok
        code = codes[at : at + 2 * tok]
        recon = jnp.dot(code, weights, preferred_element_type=F32)
        if chip == 0:
            proj = jnp.concatenate(
                [nt(v[:, half : 2 * half], weights) for v in (keep, got)], axis=0
            )
            own_recon[...] = recon
            own_proj[...] = proj
        else:
            proj = nt(src[:, half : 2 * half], weights)
            out = sends[chip - 1]
            out[:, :half] = recon.astype(BF)
            out[:, half : half + names] = proj.astype(BF)
            out[:tok, half + names :] = code[:tok, : names // 2]
            out[tok:, half + names :] = code[:tok, names // 2 :]
        totals.append(jnp.sum(code.astype(F32) * proj, axis=0, keepdims=True))
    sums[...] = jnp.concatenate(
        [totals[0] + totals[1], totals[2] + totals[3], jnp.zeros((6, names), F32)], axis=0
    )


def home_kernel(half, names, place, own_recon, own_proj, from_x, from_y, from_d, kept, send):
    tok = kept.shape[0]
    others = (from_x, from_y, from_d)
    total = own_recon[...]
    for src in others:
        total = total + src[:, :half].astype(F32)
    kept[...] = total[:tok]
    send[:, :half] = total[tok:].astype(BF)
    send[:, half : half + names] = own_proj[tok:].astype(BF)
    for i, src in enumerate(others):
        at = half + (i + 1) * names
        send[:, at : at + names] = src[tok:, half : half + names]


def final_kernel(
    ring, half, names, place, kept, got, own_proj, codes, from_x, from_y, from_d, res, dec_bias, ids,
    out_codes, out_scores, out_error,
):
    tok = kept.shape[0]
    active = ids.shape[1]
    here = pl.multiple_of(place[3] * half, 128)
    there = pl.multiple_of((1 - place[3]) * half, 128)
    for at, recon in ((here, kept[...]), (there, got[:, :half].astype(F32))):
        cols = pl.ds(at, half)
        out_error[:, cols] = (res[:, cols].astype(F32) - dec_bias[:, cols] - recon).astype(BF)
    code_src, proj_src = [codes[:tok].astype(F32)], [own_proj[:tok]]
    for src in (from_x, from_y, from_d):
        code_src.append(
            jnp.concatenate([src[:tok, half + names :], src[tok:, half + names :]], axis=1).astype(F32)
        )
        proj_src.append(src[:tok, half : half + names].astype(F32))
    proj_src = [
        v + got[:, half + i * names : half + (i + 1) * names].astype(F32)
        for i, v in enumerate(proj_src)
    ]
    lane = lax.broadcasted_iota(jnp.int32, (tok, 128), 1)
    low = lane < 64
    y = place[1]
    code_out = [jnp.zeros((tok, 128), F32)] * active
    proj_out = [jnp.zeros((tok, 128), F32)] * active
    for x_rel in range(2):
        for kk in range(ring):
            cols = slice(128 * (kk // 2), 128 * (kk // 2) + 128)
            turn = place[2] - kk
            turn = jnp.where(turn < 0, turn + ring, turn)
            block = turn * 2 + (place[0] ^ x_rel)
            pair = []
            for src in (code_src, proj_src):
                near, far = src[x_rel][:, cols], src[2 + x_rel][:, cols]
                first = jnp.where(y == 0, near, far)
                second = jnp.where(y == 0, far, near)
                if kk % 2 == 0:
                    pair.append(jnp.where(low, first, pltpu.roll(second, 64, 1)))
                else:
                    pair.append(jnp.where(low, pltpu.roll(first, 64, 1), second))
            for k in range(active):
                hit = ids[:, k : k + 1] == block
                code_out[k] = code_out[k] + jnp.where(hit, pair[0], 0.0)
                proj_out[k] = proj_out[k] + jnp.where(hit, pair[1], 0.0)
    for k in range(active):
        out_codes[:, k, :] = code_out[k].astype(BF)
        out_scores[:, k, :] = code_out[k] * proj_out[k]


def move_weights(residual, gradient, block_ids, jump_mask, encoder, enc_bias, decoder, dec_bias):
    tok, width = residual.shape
    active = block_ids.shape[1]
    lanes = jump_mask.shape[2]
    lat_count = lax.axis_size("lat")
    ring = lat_count // 2
    per = lanes // 2
    half = width // 2
    names = ring * per
    y = lax.axis_index("groups")
    lat = lax.axis_index("lat")
    s = lax.axis_index("seq")
    z, x = lat // 2, lat % 2
    place = jnp.stack([x, y, z, s]).astype(jnp.int32)

    def permute(values, to):
        pairs = []
        for gg in range(2):
            for ll in range(lat_count):
                for ss in range(2):
                    a, b, c = to(gg, ll, ss)
                    pairs.append(((gg * lat_count + ll) * 2 + ss, (a * lat_count + b) * 2 + c))
        return lax.ppermute(values, AXES, pairs)

    def by_x(v):
        return permute(v, lambda gg, ll, ss: (gg, ll ^ 1, ss))

    def by_y(v):
        return permute(v, lambda gg, ll, ss: (1 - gg, ll, ss))

    def by_xy(v):
        return permute(v, lambda gg, ll, ss: (1 - gg, ll ^ 1, ss))

    def by_core(v):
        return permute(v, lambda gg, ll, ss: (gg, ll, 1 - ss))

    def by_z(v, k):
        return permute(v, lambda gg, ll, ss: (gg, (ll + 2 * k) % lat_count, ss))

    enc_q, dec_q = pl.pallas_call(
        weights_kernel,
        grid_spec=pltpu.PrefetchScalarGridSpec(
            num_scalar_prefetch=1,
            grid=(1,),
            in_specs=[
                pl.BlockSpec((half, lanes), lambda i, p: (p[3], 0)),
                pl.BlockSpec((per, half), lambda i, p: (p[1], p[3])),
                pl.BlockSpec((1, lanes), lambda i, p: (0, 0)),
            ],
            out_specs=[
                pl.BlockSpec((per, half + 128), lambda i, p: (0, 0)),
                pl.BlockSpec((per, half), lambda i, p: (0, 0)),
            ],
        ),
        out_shape=[
            jax.ShapeDtypeStruct((per, half + 128), BF),
            jax.ShapeDtypeStruct((per, half), BF),
        ],
        compiler_params=pltpu.CompilerParams(vmem_limit_bytes=32 << 20),
    )(place, encoder, decoder, enc_bias.reshape(1, lanes))
    enc_parts, dec_parts = [enc_q], [dec_q]
    for _ in range(ring - 1):
        enc_parts.append(by_z(enc_parts[-1], 1))
        dec_parts.append(by_z(dec_parts[-1], 1))

    lead = width + 4 * names
    keep, send = call(
        functools.partial(tokens_kernel, ring),
        [((tok, lead), BF)] * 2,
        place, residual, gradient, block_ids, jump_mask,
    )
    got = by_core(send)
    to_x, to_y, to_d = call(
        rows_kernel, [((2 * tok, width + names), BF)] * 3, place, keep, got
    )
    rows = (keep, got, by_x(to_x), by_y(to_y), by_xy(to_d))

    (part,) = call(
        functools.partial(preact_kernel, ring, half),
        [((8 * tok, names), F32)], place, *rows, *enc_parts,
    )
    (codes,) = call(codes_kernel, [((8 * tok, names), BF)], place, part, by_core(part), *rows)
    out_lanes = half + names + names // 2
    own_recon, own_proj, sums, to_x, to_y, to_d = call(
        functools.partial(recon_kernel, ring, half),
        [((2 * tok, half), F32), ((2 * tok, names), F32), ((8, names), F32)]
        + [((2 * tok, out_lanes), BF)] * 3,
        place, codes, *rows, *dec_parts,
    )
    from_d = by_xy(to_d)
    from_x = by_x(to_x)
    from_y = by_y(to_y)

    total = sums[:2, :per]
    for k in range(1, ring):
        total = total + by_z(sums, -k)[:2, per * k : per * k + per]
    other = by_y(total[1])
    both = jnp.where(
        y == 0, jnp.concatenate([total[0], other]), jnp.concatenate([other, total[0]])
    ).reshape(2, per)
    mine = jnp.where(s == 0, both[0], both[1])
    theirs = jnp.where(s == 0, both[1], both[0])
    factor = (tok * lat_count * 2 * active / lat_count) ** (-0.5)
    latent_totals = (mine + by_core(theirs)) * factor

    kept, send = call(
        functools.partial(home_kernel, half, names),
        [((tok, half), F32), ((tok, half + 4 * names), BF)],
        place, own_recon, own_proj, from_x, from_y, from_d,
    )
    latent_codes, attribution, recon_error = call(
        functools.partial(final_kernel, ring, half, names),
        [((tok, active, lanes), BF), ((tok, active, lanes), F32), ((tok, width), BF)],
        place, kept, by_core(send), own_proj, codes, from_x, from_y, from_d,
        residual, dec_bias.reshape(1, width), block_ids,
    )
    return (latent_codes, attribution, recon_error, latent_totals)


def solution(mesh):
    sizes = dict(mesh.shape)

    def on_device(residual, gradient, block_ids, jump_mask, encoder, enc_bias, decoder, dec_bias):
        lanes = jump_mask.shape[2]
        small = (
            sizes["groups"] == 2
            and sizes["seq"] == 2
            and sizes["lat"] in (4, 8, 16)
            and encoder.shape[1] == lanes
            and lanes == 128
            and residual.shape[0] % 16 == 0
            and residual.shape[1] % 256 == 0
        )
        body = move_weights if small else move_tokens
        return body(
            residual, gradient, block_ids, jump_mask, encoder, enc_bias, decoder, dec_bias
        )

    rows = P(("groups", "lat", "seq"), None)
    cubes = P(("groups", "lat", "seq"), None, None)
    return jax.shard_map(
        on_device,
        mesh=mesh,
        in_specs=(rows, rows, rows, cubes, P(None, "lat"), P("lat"), P("lat", None), P()),
        out_specs=(cubes, cubes, rows, P(("groups", "lat", "seq"))),
        check_vma=False,
    )
```

```python
import functools

import jax
import jax.numpy as jnp
from jax import lax
from jax.experimental import pallas as pl
from jax.experimental.pallas import tpu as pltpu
from jax.sharding import PartitionSpec as P

AXES = ("groups", "lat", "seq")


def place_rows(values, source, filled, leading):
    picked = jnp.where(filled[:, None], values[source], jnp.zeros((), values.dtype))
    return picked.reshape(leading + (values.shape[-1],))


def move_tokens(residual, gradient, block_ids, jump_mask, encoder, enc_bias, decoder, dec_bias):
    tok_rows, width = residual.shape
    active = block_ids.shape[1]
    lanes = jump_mask.shape[2]
    lat_count = lax.axis_size("lat")
    seq_count = lax.axis_size("seq")
    local_blocks = encoder.shape[1] // lanes
    block_count = local_blocks * lat_count
    capacity = max(
        2, min(tok_rows, (3 * tok_rows * active + 2 * block_count - 1) // (2 * block_count))
    )
    slot_count = tok_rows * active
    flat_blocks = block_ids.reshape(slot_count)
    one_hot = (flat_blocks[:, None] == jnp.arange(block_count, dtype=jnp.int32)[None, :]).astype(
        jnp.int32
    )
    earlier = jnp.sum(jnp.cumsum(one_hot, axis=0) * one_hot, axis=1) - 1
    slot_id = flat_blocks * capacity + earlier
    owner_row = (
        jnp.zeros((block_count * capacity,), jnp.int32)
        .at[slot_id]
        .set(jnp.arange(slot_count, dtype=jnp.int32) + 1)
    )
    filled = owner_row > 0
    slot_source = jnp.maximum(owner_row - 1, 0)
    token_source = slot_source // active
    leading = (lat_count, local_blocks, capacity)
    enc_blocks = encoder.reshape(width, local_blocks, lanes)
    dec_blocks = decoder.reshape(local_blocks, lanes, width)
    bias_blocks = enc_bias.reshape(1, local_blocks, 1, lanes)
    mask_values = jump_mask.astype(jnp.float32)
    total_tokens = tok_rows * lat_count * seq_count
    factor = (total_tokens * active / block_count) ** (-0.5)

    def gather_home(slotted):
        last = slotted.shape[-1]
        return slotted.reshape(block_count * capacity, last)[slot_id].reshape(
            tok_rows, active, last
        )

    def swap(values):
        return lax.all_to_all(values, "lat", split_axis=0, concat_axis=0, tiled=True)

    residual_slots = place_rows(residual, token_source, filled, leading)
    gradient_slots = place_rows(gradient, token_source, filled, leading)
    preact = jnp.einsum(
        "sbcd,dbj->sbcj", swap(residual_slots), enc_blocks, preferred_element_type=jnp.float32
    )
    preact = swap((preact + bias_blocks).astype(jnp.bfloat16)).astype(jnp.float32)
    latent_codes = (gather_home(preact) * mask_values).astype(jnp.bfloat16)
    code_slots = place_rows(latent_codes.reshape(slot_count, lanes), slot_source, filled, leading)
    code_data = swap(code_slots)
    grad_data = swap(gradient_slots)
    score_data = code_data.astype(jnp.float32) * jnp.einsum(
        "sbcd,bjd->sbcj", grad_data, dec_blocks, preferred_element_type=jnp.float32
    )
    recon_data = jnp.einsum(
        "sbcj,bjd->sbcd", code_data, dec_blocks, preferred_element_type=jnp.float32
    )
    recon_home = gather_home(swap(recon_data.astype(jnp.bfloat16)))
    attribution = gather_home(swap(score_data))
    recon_error = (
        residual.astype(jnp.float32) - dec_bias - jnp.sum(recon_home.astype(jnp.float32), axis=1)
    ).astype(jnp.bfloat16)
    term = jnp.dot(
        one_hot.T.astype(jnp.float32),
        attribution.reshape(slot_count, lanes),
        precision=lax.Precision.HIGHEST,
    )
    latent_totals = (
        lax.psum_scatter(
            term.reshape(block_count * lanes), ("lat", "seq"), scatter_dimension=0, tiled=True
        )
        * factor
    )
    return (latent_codes, attribution, recon_error, latent_totals)


BF = jnp.bfloat16
F32 = jnp.float32


def nt(a, b):
    return lax.dot_general(a, b, (((1,), (1,)), ((), ())), preferred_element_type=F32)


def call(kernel, outs, *args, far=(), scratch=(), vmem=48, flops=0, size=1 << 20):
    specs = [pl.BlockSpec(memory_space=pltpu.SMEM)]
    for i in range(1, len(args)):
        specs.append(pl.BlockSpec(memory_space=pl.ANY if i in far else pltpu.VMEM))
    return pl.pallas_call(
        kernel,
        in_specs=specs,
        out_specs=[pl.BlockSpec(memory_space=pltpu.VMEM)] * len(outs),
        out_shape=[jax.ShapeDtypeStruct(*o) for o in outs],
        scratch_shapes=list(scratch),
        compiler_params=pltpu.CompilerParams(vmem_limit_bytes=vmem << 20),
        cost_estimate=pl.CostEstimate(flops=flops, bytes_accessed=size, transcendentals=0),
    )(*args)


def weights_kernel(place, enc, dec, bias, out, enc_half, sem):
    lanes = enc.shape[1]
    half = enc_half.shape[0]
    per = out.shape[0]
    cols = pl.ds(pl.multiple_of(place[3] * half, 128), half)
    get_enc = pltpu.make_async_copy(enc.at[cols, :], enc_half, sem.at[0])
    get_dec = pltpu.make_async_copy(
        dec.at[pl.ds(pl.multiple_of(place[1] * per, 16), per), cols],
        out.at[:, pl.ds(half + 128, half)],
        sem.at[1],
    )
    get_enc.start()
    get_dec.start()
    row = lax.broadcasted_iota(jnp.int32, (per, lanes), 0)
    lane = lax.broadcasted_iota(jnp.int32, (per, lanes), 1)
    pick = (lane == row + per * place[1]).astype(BF)
    b = bias[...]
    hi = b.astype(BF).astype(F32)
    mid = (b - hi).astype(BF).astype(F32)
    low = b - hi - mid
    term = lax.broadcasted_iota(jnp.int32, (lanes, lanes), 0)
    terms = jnp.where(term == 0, hi, jnp.where(term == 1, mid, jnp.where(term == 2, low, 0.0)))
    out[:, half : half + 128] = nt(pick, terms.astype(BF)).astype(BF)
    get_enc.wait()
    out[:, :half] = nt(pick, enc_half[...]).astype(BF)
    get_dec.wait()


def split_kernel(place, both, enc_out, dec_out):
    enc_out[...] = both[:, : enc_out.shape[1]]
    dec_out[...] = both[:, enc_out.shape[1] :]


def after_kernel(place, values, waited, out):
    out[...] = values[...]


def target_block(lane, m, place, x_rel, ring):
    turn = place[2] - 2 * m - (lane >= 64).astype(jnp.int32)
    turn = jnp.where(turn < 0, turn + ring, turn)
    return turn * 2 + (place[0] ^ x_rel)


def tokens_kernel(ring, place, res, grad, ids, jump, keep, send, sem):
    tok, width = res.shape
    half = width // 2
    active = ids.shape[0]
    copies = []
    for i, src in enumerate((res, grad)):
        for j, out in enumerate((keep, send)):
            side = place[3] if j == 0 else 1 - place[3]
            copies.append(
                pltpu.make_async_copy(
                    src.at[:, pl.ds(pl.multiple_of(side * half, 128), half)],
                    out.at[:, pl.ds(i * half, half)],
                    sem.at[2 * i + j],
                )
            )
    for copy in copies:
        copy.start()
    names = ids[...].T
    lane = lax.broadcasted_iota(jnp.int32, (tok, 128), 1)
    low = lane < 64
    plain = [jump[:, k, :] for k in range(active)]
    moved = [pltpu.roll(v, 64, 1) for v in plain]
    for dest in range(4):
        x_rel, y_rel = dest % 2, dest // 2
        first = (place[1] ^ y_rel) == 0
        for m in range(ring // 2):
            tgt = target_block(lane, m, place, x_rel, ring)
            total = jnp.zeros((tok, 128), jnp.int32)
            for k in range(active):
                value = jnp.where(low == first, plain[k], moved[k])
                total = total + jnp.where(names[:, k : k + 1] == tgt, value, 0)
            at = width + (dest * (ring // 2) + m) * 128
            out = total.astype(F32).astype(BF)
            keep[:, at : at + 128] = out
            send[:, at : at + 128] = out
    for copy in copies:
        copy.wait()


def rows_kernel(place, keep, got, *outs):
    tok = keep.shape[0]
    width = outs[0].shape[1]
    names = (keep.shape[1] - width) // 3
    width = width - names
    for dest, out in enumerate(outs):
        at = width + (dest + 1) * names
        for i, src in enumerate((keep, got)):
            out[i * tok : (i + 1) * tok, :width] = src[:, :width]
            out[i * tok : (i + 1) * tok, width:] = src[:, at : at + names]


def preact_kernel(ring, half, place, keep, got, from_x, from_y, from_d, *refs):
    parts, out = refs[:ring], refs[ring]
    tok = keep.shape[0]
    per = parts[0].shape[0]
    weights = jnp.concatenate([p[:, :half] for p in parts], axis=0)
    extra = jnp.concatenate([p[:, half : half + 128] for p in parts], axis=0)
    ones = jnp.where(place[3] == 0, 1.0, 0.0) * jnp.ones((8, 128), F32)
    bias = nt(ones.astype(BF), extra)[:1]
    at = 0
    for src in (keep, got, from_x, from_y, from_d):
        n = src.shape[0]
        out[at : at + n] = nt(src[:, :half], weights) + bias
        at += n


def codes_kernel(place, mine, other, keep, got, from_x, from_y, from_d, out):
    tok = keep.shape[0]
    names = out.shape[1]
    base = keep.shape[1] - 4 * names
    for chip, src in enumerate((None, from_x, from_y, from_d)):
        for i in range(2):
            at = (2 * chip + i) * tok
            swapped = (2 * chip + 1 - i) * tok
            if chip == 0:
                mask = (keep, got)[i][:, base : base + names]
            else:
                mask = src[i * tok : (i + 1) * tok, base:]
            total = mine[at : at + tok] + other[swapped : swapped + tok]
            out[at : at + tok] = (total * mask.astype(F32)).astype(BF)


def recon_kernel(ring, half, place, codes, keep, got, from_x, from_y, from_d, *refs):
    parts = refs[:ring]
    own_recon, own_proj, sums = refs[ring : ring + 3]
    sends = refs[ring + 3 :]
    tok = keep.shape[0]
    names = codes.shape[1]
    weights = jnp.concatenate([p[:, p.shape[1] - half :] for p in parts], axis=0)
    totals = []
    for chip, src in enumerate((None, from_x, from_y, from_d)):
        at = chip * 2 * tok
        code = codes[at : at + 2 * tok]
        recon = jnp.dot(code, weights, preferred_element_type=F32)
        if chip == 0:
            proj = jnp.concatenate(
                [nt(v[:, half : 2 * half], weights) for v in (keep, got)], axis=0
            )
            own_recon[...] = recon
            own_proj[...] = proj
        else:
            proj = nt(src[:, half : 2 * half], weights)
            out = sends[chip - 1]
            out[:, :half] = recon.astype(BF)
            out[:, half : half + names] = proj.astype(BF)
            out[:tok, half + names :] = code[:tok, : names // 2]
            out[tok:, half + names :] = code[:tok, names // 2 :]
        totals.append(jnp.sum(code.astype(F32) * proj, axis=0, keepdims=True))
    sums[...] = jnp.concatenate(
        [totals[0] + totals[1], totals[2] + totals[3], jnp.zeros((6, names), F32)], axis=0
    )


def home_kernel(half, names, place, own_recon, own_proj, from_x, from_y, from_d, kept, send):
    tok = kept.shape[0]
    others = (from_x, from_y, from_d)
    total = own_recon[...]
    for src in others:
        total = total + src[:, :half].astype(F32)
    kept[...] = total[:tok]
    send[:, :half] = total[tok:].astype(BF)
    send[:, half : half + names] = own_proj[tok:].astype(BF)
    for i, src in enumerate(others):
        at = half + (i + 1) * names
        send[:, at : at + names] = src[tok:, half : half + names]


def final_kernel(
    ring, half, names, place, kept, got, own_proj, codes, from_x, from_y, from_d, res, dec_bias, ids,
    out_codes, out_scores, out_error,
):
    tok = kept.shape[0]
    active = ids.shape[0]
    named = ids[...].T
    here = pl.multiple_of(place[3] * half, 128)
    there = pl.multiple_of((1 - place[3]) * half, 128)
    for at, recon in ((here, kept[...]), (there, got[:, :half].astype(F32))):
        cols = pl.ds(at, half)
        out_error[:, cols] = (res[:, cols].astype(F32) - dec_bias[:, cols] - recon).astype(BF)
    code_src, proj_src = [codes[:tok].astype(F32)], [own_proj[:tok]]
    for src in (from_x, from_y, from_d):
        code_src.append(
            jnp.concatenate([src[:tok, half + names :], src[tok:, half + names :]], axis=1).astype(F32)
        )
        proj_src.append(src[:tok, half : half + names].astype(F32))
    proj_src = [
        v + got[:, half + i * names : half + (i + 1) * names].astype(F32)
        for i, v in enumerate(proj_src)
    ]
    lane = lax.broadcasted_iota(jnp.int32, (tok, 128), 1)
    low = lane < 64
    y = place[1]
    code_out = [jnp.zeros((tok, 128), F32)] * active
    proj_out = [jnp.zeros((tok, 128), F32)] * active
    for x_rel in range(2):
        for kk in range(ring):
            cols = slice(128 * (kk // 2), 128 * (kk // 2) + 128)
            turn = place[2] - kk
            turn = jnp.where(turn < 0, turn + ring, turn)
            block = turn * 2 + (place[0] ^ x_rel)
            pair = []
            for src in (code_src, proj_src):
                near, far = src[x_rel][:, cols], src[2 + x_rel][:, cols]
                first = jnp.where(y == 0, near, far)
                second = jnp.where(y == 0, far, near)
                if kk % 2 == 0:
                    pair.append(jnp.where(low, first, pltpu.roll(second, 64, 1)))
                else:
                    pair.append(jnp.where(low, pltpu.roll(first, 64, 1), second))
            for k in range(active):
                hit = named[:, k : k + 1] == block
                code_out[k] = code_out[k] + jnp.where(hit, pair[0], 0.0)
                proj_out[k] = proj_out[k] + jnp.where(hit, pair[1], 0.0)
    for k in range(active):
        out_codes[:, k, :] = code_out[k].astype(BF)
        out_scores[:, k, :] = code_out[k] * proj_out[k]


def move_weights(residual, gradient, block_ids, jump_mask, encoder, enc_bias, decoder, dec_bias):
    tok, width = residual.shape
    active = block_ids.shape[1]
    lanes = jump_mask.shape[2]
    lat_count = lax.axis_size("lat")
    ring = lat_count // 2
    per = lanes // 2
    half = width // 2
    names = ring * per
    y = lax.axis_index("groups")
    lat = lax.axis_index("lat")
    s = lax.axis_index("seq")
    z, x = lat // 2, lat % 2
    place = jnp.stack([x, y, z, s]).astype(jnp.int32)

    def permute(values, to):
        pairs = []
        for gg in range(2):
            for ll in range(lat_count):
                for ss in range(2):
                    a, b, c = to(gg, ll, ss)
                    pairs.append(((gg * lat_count + ll) * 2 + ss, (a * lat_count + b) * 2 + c))
        return lax.ppermute(values, AXES, pairs)

    def by_x(v):
        return permute(v, lambda gg, ll, ss: (gg, ll ^ 1, ss))

    def by_y(v):
        return permute(v, lambda gg, ll, ss: (1 - gg, ll, ss))

    def by_xy(v):
        return permute(v, lambda gg, ll, ss: (1 - gg, ll ^ 1, ss))

    def by_core(v):
        return permute(v, lambda gg, ll, ss: (gg, ll, 1 - ss))

    def by_z(v, k):
        return permute(v, lambda gg, ll, ss: (gg, (ll + 2 * k) % lat_count, ss))

    (own,) = call(
        weights_kernel,
        [((per, 2 * half + 128), BF)],
        place, encoder, decoder, enc_bias.reshape(1, lanes),
        far=(1, 2),
        scratch=[pltpu.VMEM((half, lanes), BF), pltpu.SemaphoreType.DMA((2,))],
        vmem=56,
    )
    first = by_z(own, 1)
    enc_next, dec_next = call(
        split_kernel, [((per, half + 128), BF), ((per, half), BF)], place, first
    )
    enc_parts, dec_parts = [own, first], [own, first]
    for _ in range(ring - 2):
        enc_next, dec_next = by_z(enc_next, 1), by_z(dec_next, 1)
        enc_parts.append(enc_next)
        dec_parts.append(dec_next)

    lead = width + 4 * names
    keep, send = call(
        functools.partial(tokens_kernel, ring),
        [((tok, lead), BF)] * 2,
        place, residual, gradient, block_ids.T, jump_mask,
        far=(1, 2),
        scratch=[pltpu.SemaphoreType.DMA((4,))],
        vmem=56,
    )
    got = by_core(send)
    to_x, to_y, to_d = call(
        rows_kernel, [((2 * tok, width + names), BF)] * 3, place, keep, got
    )
    rows = (keep, got, by_x(to_x), by_y(to_y), by_xy(to_d))

    (part,) = call(
        functools.partial(preact_kernel, ring, half),
        [((8 * tok, names), F32)], place, *rows, *enc_parts,
    )
    (codes,) = call(codes_kernel, [((8 * tok, names), BF)], place, part, by_core(part), *rows)
    out_lanes = half + names + names // 2
    own_recon, own_proj, sums, to_x, to_y, to_d = call(
        functools.partial(recon_kernel, ring, half),
        [((2 * tok, half), F32), ((2 * tok, names), F32), ((8, names), F32)]
        + [((2 * tok, out_lanes), BF)] * 3,
        place, codes, *rows, *dec_parts,
    )
    from_d = by_xy(to_d)
    from_x = by_x(to_x)
    from_y = by_y(to_y)

    (sums,) = call(after_kernel, [(sums.shape, F32)], place, sums, from_x, far=(2,))
    total = sums[:2, :per]
    for k in range(1, ring):
        total = total + by_z(sums, -k)[:2, per * k : per * k + per]
    row = jnp.where(y == s, total[0], total[1])
    rest = jnp.where(y == s, total[1], total[0])
    factor = (tok * lat_count * 2 * active / lat_count) ** (-0.5)
    latent_totals = (
        permute(row, lambda gg, ll, ss: (ss, ll, gg))
        + permute(rest, lambda gg, ll, ss: (1 - ss, ll, gg))
    ) * factor

    kept, send = call(
        functools.partial(home_kernel, half, names),
        [((tok, half), F32), ((tok, half + 4 * names), BF)],
        place, own_recon, own_proj, from_x, from_y, from_d,
    )
    latent_codes, attribution, recon_error = call(
        functools.partial(final_kernel, ring, half, names),
        [((tok, active, lanes), BF), ((tok, active, lanes), F32), ((tok, width), BF)],
        place, kept, by_core(send), own_proj, codes, from_x, from_y, from_d,
        residual, dec_bias.reshape(1, width), block_ids.T,
    )
    return (latent_codes, attribution, recon_error, latent_totals)


def solution(mesh):
    sizes = dict(mesh.shape)

    def on_device(residual, gradient, block_ids, jump_mask, encoder, enc_bias, decoder, dec_bias):
        lanes = jump_mask.shape[2]
        small = (
            sizes["groups"] == 2
            and sizes["seq"] == 2
            and sizes["lat"] in (4, 8, 16)
            and encoder.shape[1] == lanes
            and lanes == 128
            and residual.shape[0] % 16 == 0
            and residual.shape[1] % 256 == 0
        )
        body = move_weights if small else move_tokens
        return body(
            residual, gradient, block_ids, jump_mask, encoder, enc_bias, decoder, dec_bias
        )

    rows = P(("groups", "lat", "seq"), None)
    cubes = P(("groups", "lat", "seq"), None, None)
    return jax.shard_map(
        on_device,
        mesh=mesh,
        in_specs=(rows, rows, rows, cubes, P(None, "lat"), P("lat"), P("lat", None), P()),
        out_specs=(cubes, cubes, rows, P(("groups", "lat", "seq"))),
        check_vma=False,
    )
```

```python
import functools

import jax
import jax.numpy as jnp
from jax import lax
from jax.experimental import pallas as pl
from jax.experimental.pallas import tpu as pltpu
from jax.sharding import PartitionSpec as P

AXES = ("groups", "lat", "seq")


def place_rows(values, source, filled, leading):
    picked = jnp.where(filled[:, None], values[source], jnp.zeros((), values.dtype))
    return picked.reshape(leading + (values.shape[-1],))


def move_tokens(residual, gradient, block_ids, jump_mask, encoder, enc_bias, decoder, dec_bias):
    tok_rows, width = residual.shape
    active = block_ids.shape[1]
    lanes = jump_mask.shape[2]
    lat_count = lax.axis_size("lat")
    seq_count = lax.axis_size("seq")
    local_blocks = encoder.shape[1] // lanes
    block_count = local_blocks * lat_count
    capacity = max(
        2, min(tok_rows, (3 * tok_rows * active + 2 * block_count - 1) // (2 * block_count))
    )
    slot_count = tok_rows * active
    flat_blocks = block_ids.reshape(slot_count)
    one_hot = (flat_blocks[:, None] == jnp.arange(block_count, dtype=jnp.int32)[None, :]).astype(
        jnp.int32
    )
    earlier = jnp.sum(jnp.cumsum(one_hot, axis=0) * one_hot, axis=1) - 1
    slot_id = flat_blocks * capacity + earlier
    owner_row = (
        jnp.zeros((block_count * capacity,), jnp.int32)
        .at[slot_id]
        .set(jnp.arange(slot_count, dtype=jnp.int32) + 1)
    )
    filled = owner_row > 0
    slot_source = jnp.maximum(owner_row - 1, 0)
    token_source = slot_source // active
    leading = (lat_count, local_blocks, capacity)
    enc_blocks = encoder.reshape(width, local_blocks, lanes)
    dec_blocks = decoder.reshape(local_blocks, lanes, width)
    bias_blocks = enc_bias.reshape(1, local_blocks, 1, lanes)
    mask_values = jump_mask.astype(jnp.float32)
    total_tokens = tok_rows * lat_count * seq_count
    factor = (total_tokens * active / block_count) ** (-0.5)

    def gather_home(slotted):
        last = slotted.shape[-1]
        return slotted.reshape(block_count * capacity, last)[slot_id].reshape(
            tok_rows, active, last
        )

    def swap(values):
        return lax.all_to_all(values, "lat", split_axis=0, concat_axis=0, tiled=True)

    residual_slots = place_rows(residual, token_source, filled, leading)
    gradient_slots = place_rows(gradient, token_source, filled, leading)
    preact = jnp.einsum(
        "sbcd,dbj->sbcj", swap(residual_slots), enc_blocks, preferred_element_type=jnp.float32
    )
    preact = swap((preact + bias_blocks).astype(jnp.bfloat16)).astype(jnp.float32)
    latent_codes = (gather_home(preact) * mask_values).astype(jnp.bfloat16)
    code_slots = place_rows(latent_codes.reshape(slot_count, lanes), slot_source, filled, leading)
    code_data = swap(code_slots)
    grad_data = swap(gradient_slots)
    score_data = code_data.astype(jnp.float32) * jnp.einsum(
        "sbcd,bjd->sbcj", grad_data, dec_blocks, preferred_element_type=jnp.float32
    )
    recon_data = jnp.einsum(
        "sbcj,bjd->sbcd", code_data, dec_blocks, preferred_element_type=jnp.float32
    )
    recon_home = gather_home(swap(recon_data.astype(jnp.bfloat16)))
    attribution = gather_home(swap(score_data))
    recon_error = (
        residual.astype(jnp.float32) - dec_bias - jnp.sum(recon_home.astype(jnp.float32), axis=1)
    ).astype(jnp.bfloat16)
    term = jnp.dot(
        one_hot.T.astype(jnp.float32),
        attribution.reshape(slot_count, lanes),
        precision=lax.Precision.HIGHEST,
    )
    latent_totals = (
        lax.psum_scatter(
            term.reshape(block_count * lanes), ("lat", "seq"), scatter_dimension=0, tiled=True
        )
        * factor
    )
    return (latent_codes, attribution, recon_error, latent_totals)


BF = jnp.bfloat16
F32 = jnp.float32


def nt(a, b):
    return lax.dot_general(a, b, (((1,), (1,)), ((), ())), preferred_element_type=F32)


def place_here():
    lat = lax.axis_index("lat")
    return lax.rem(lat, 2), lax.axis_index("groups"), lax.div(lat, 2), lax.axis_index("seq")


def call(kernel, outs, *args, far=(), scratch=(), vmem=24):
    return pl.pallas_call(
        kernel,
        in_specs=[
            pl.BlockSpec(memory_space=pl.ANY if i in far else pltpu.VMEM) for i in range(len(args))
        ],
        out_specs=[pl.BlockSpec(memory_space=pltpu.VMEM)] * len(outs),
        out_shape=[jax.ShapeDtypeStruct(*o) for o in outs],
        scratch_shapes=list(scratch),
        compiler_params=pltpu.CompilerParams(vmem_limit_bytes=vmem << 20),
    )(*args)


def pick_latents(per, lanes, y):
    row = lax.broadcasted_iota(jnp.int32, (per, lanes), 0)
    lane = lax.broadcasted_iota(jnp.int32, (per, lanes), 1)
    return (lane == row + per * y).astype(BF)


def weights_kernel(enc, dec, bias, out, enc_half, sem):
    _, y, _, s = place_here()
    lanes = enc.shape[1]
    half = enc_half.shape[0]
    per = out.shape[0]
    cols = pl.ds(pl.multiple_of(s * half, 128), half)
    get_enc = pltpu.make_async_copy(enc.at[cols, :], enc_half, sem.at[0])
    get_dec = pltpu.make_async_copy(
        dec.at[pl.ds(pl.multiple_of(y * per, 16), per), cols],
        out.at[:, pl.ds(half + 128, half)],
        sem.at[1],
    )
    get_enc.start()
    get_dec.start()
    pick = pick_latents(per, lanes, y)
    b = bias[...]
    hi = b.astype(BF).astype(F32)
    mid = (b - hi).astype(BF).astype(F32)
    low = b - hi - mid
    term = lax.broadcasted_iota(jnp.int32, (lanes, lanes), 0)
    terms = jnp.where(term == 0, hi, jnp.where(term == 1, mid, jnp.where(term == 2, low, 0.0)))
    out[:, half : half + 128] = nt(pick, terms.astype(BF)).astype(BF)
    get_enc.wait()
    out[:, :half] = nt(pick, enc_half[...]).astype(BF)
    get_dec.wait()


def totals_kernel(per, early, one, two, three, row, rest):
    _, y, _, s = place_here()
    total = early[:2, :per] + one[:2, per : 2 * per] + two[:2, :per] + three[:2, 3 * per :]
    row[...] = jnp.where(y == s, total[:1], total[1:])
    rest[...] = jnp.where(y == s, total[1:], total[:1])


def target_block(lane, m, x, z, ring):
    turn = z - 2 * m - (lane >= 64).astype(jnp.int32)
    turn = jnp.where(turn < 0, turn + ring, turn)
    return turn * 2 + x


def tokens_kernel(ring, res, grad, ids, jump, _, to_x, to_y, to_d, own_mask, sem):
    x, y, z, _ = place_here()
    tok, width = res.shape
    active = ids.shape[0]
    outs = (to_x, to_y, to_d)
    copies = []
    for i, src in enumerate((res, grad)):
        for j, out in enumerate(outs):
            copies.append(
                pltpu.make_async_copy(src, out.at[:, pl.ds(i * width, width)], sem.at[3 * i + j])
            )
    for copy in copies:
        copy.start()
    names = ids[...].T
    names = [jnp.broadcast_to(names[:, k : k + 1], (tok, 128)) for k in range(active)]
    lane = lax.broadcasted_iota(jnp.int32, (tok, 128), 1)
    low = lane < 64
    plain = [jump[:, k, :] for k in range(active)]
    moved = [pltpu.roll(v, 64, 1) for v in plain]
    for dest in range(4):
        x_rel, y_rel = dest % 2, dest // 2
        first = (y ^ y_rel) == 0
        for m in range(ring // 2):
            tgt = target_block(lane, m, x ^ x_rel, z, ring)
            total = jnp.zeros((tok, 128), jnp.int32)
            for k in range(active):
                value = jnp.where(low == first, plain[k], moved[k])
                total = total + jnp.where(names[k] == tgt, value, 0)
            out = total.astype(F32).astype(BF)
            if dest == 0:
                own_mask[:, m * 128 : m * 128 + 128] = out
            else:
                at = 2 * width + m * 128
                outs[dest - 1][:, at : at + 128] = out
    for copy in copies:
        copy.wait()


def group_sums(scores):
    half = scores.shape[0] // 2
    near = jnp.sum(scores[:half], axis=0, keepdims=True)
    far = jnp.sum(scores[half:], axis=0, keepdims=True)
    return jnp.concatenate([near, far, jnp.zeros((6, scores.shape[1]), F32)], axis=0)


def early_kernel(
    own, own_mask, from_x, from_y, from_d, enc, dec, mine_0, mine_1, other_1, mine_3, other_3,
    rows, mask, recon, codes, scores, sums, enc_half, other_0, sem,
):
    _, y, _, s = place_here()
    tok = own.shape[0]
    per, lanes = mine_0.shape[0], enc.shape[1]
    half = enc_half.shape[0]
    width = 2 * half
    far = pl.ds(pl.multiple_of((1 - s) * half, 128), half)
    get_enc = pltpu.make_async_copy(enc.at[far, :], enc_half, sem.at[0])
    get_dec = pltpu.make_async_copy(
        dec.at[pl.ds(pl.multiple_of(y * per, 16), per), far],
        other_0.at[:, pl.ds(half + 128, half)],
        sem.at[1],
    )
    get_enc.start()
    get_dec.start()
    for i, src in enumerate((own, from_x, from_y, from_d)):
        at = slice(i * tok, (i + 1) * tok)
        mask[at] = own_mask[...] if i == 0 else src[:, 2 * width :]
        for j in range(4):
            side = s if j % 2 == 0 else 1 - s
            cols = pl.ds(pl.multiple_of(width * (j // 2) + side * half, 128), half)
            rows[at, j * half : (j + 1) * half] = src[:, cols]
    get_enc.wait()
    other_0[:, :half] = nt(pick_latents(per, lanes, y), enc_half[...]).astype(BF)
    get_dec.wait()
    blank = jnp.zeros((per, half), BF)
    sides = ((mine_0, mine_1, mine_3), (other_0, other_1, other_3))

    def stack(parts, at, n):
        return jnp.concatenate(
            [parts[0][:, at : at + n], parts[1][:, at : at + n], blank[:, :n], parts[2][:, at : at + n]],
            axis=0,
        )

    preact = nt(jnp.ones((8, 128), BF), stack(sides[0], half, 128))[:1]
    for j, parts in enumerate(sides):
        preact = preact + nt(rows[:, j * half : (j + 1) * half], stack(parts, 0, half))
    code = (preact * mask[...].astype(F32)).astype(BF)
    codes[...] = code
    proj = jnp.zeros(code.shape, F32)
    for j, parts in enumerate(sides):
        weights = stack(parts, half + 128, half)
        proj = proj + nt(rows[:, (2 + j) * half : (3 + j) * half], weights)
        recon[:, j * half : (j + 1) * half] = jnp.dot(code, weights, preferred_element_type=F32)
    score = code.astype(F32) * proj
    scores[...] = score
    sums[...] = group_sums(score)


def late_kernel(
    rows, mask, recon, codes, scores, mine_2, other_2,
    own_recon, own_codes, own_scores, to_x, to_y, to_d, sums,
):
    _, _, _, s = place_here()
    per = mine_2.shape[0]
    tok = own_codes.shape[0]
    width = own_recon.shape[1]
    half = width // 2
    names = codes.shape[1]
    blank = jnp.zeros((per, half), BF)
    sides = (mine_2, other_2)

    def stack(part, at, n):
        return jnp.concatenate([part[:, at : at + n], blank[:, :n]], axis=0)

    preact = nt(jnp.ones((8, 128), BF), stack(mine_2, half, 128))[:1]
    for j, part in enumerate(sides):
        preact = preact + nt(rows[:, j * half : (j + 1) * half], stack(part, 0, half))
    code = (preact * mask[:, 2 * per :].astype(F32)).astype(BF)
    proj = jnp.zeros(code.shape, F32)
    outs = (own_recon, to_x, to_y, to_d)
    for j, part in enumerate(sides):
        weights = stack(part, half + 128, half)
        proj = proj + nt(rows[:, (2 + j) * half : (3 + j) * half], weights)
        total = recon[:, j * half : (j + 1) * half] + jnp.dot(
            code, weights, preferred_element_type=F32
        )
        cols = pl.ds(pl.multiple_of((s if j == 0 else 1 - s) * half, 128), half)
        for i, out in enumerate(outs):
            out[:, cols] = total[i * tok : (i + 1) * tok].astype(out.dtype)
    score = code.astype(F32) * proj
    sums[...] = group_sums(score)
    all_codes = jnp.concatenate([codes[:, : 2 * per], code + codes[:, 2 * per :]], axis=1)
    all_scores = jnp.concatenate([scores[:, : 2 * per], score + scores[:, 2 * per :]], axis=1)
    own_codes[...] = all_codes[:tok]
    own_scores[...] = all_scores[:tok]
    for i, out in enumerate((to_x, to_y, to_d)):
        at = slice((i + 1) * tok, (i + 2) * tok)
        out[:, width : width + names] = all_codes[at]
        out[:, width + names :] = all_scores[at].astype(BF)


def final_kernel(
    ring, factor, own_recon, own_codes, own_scores, from_x, from_y, from_d, own, dec_bias, ids, row, rest,
    out_codes, out_scores, out_error, out_totals,
):
    x, y, z, _ = place_here()
    out_totals[...] = (row[...] + rest[...]) * factor
    tok, width = own_recon.shape
    names = own_codes.shape[1]
    active = ids.shape[0]
    named = ids[...].T
    named = [jnp.broadcast_to(named[:, k : k + 1], (tok, 128)) for k in range(active)]
    others = (from_x, from_y, from_d)
    recon = own_recon[...]
    for src in others:
        recon = recon + src[:, :width].astype(F32)
    out_error[...] = (own[:, :width].astype(F32) - dec_bias[...] - recon).astype(BF)
    code_src = [own_codes[...].astype(F32)]
    score_src = [own_scores[...]]
    for src in others:
        code_src.append(src[:, width : width + names].astype(F32))
        score_src.append(src[:, width + names :].astype(F32))
    lane = lax.broadcasted_iota(jnp.int32, (tok, 128), 1)
    low = lane < 64
    code_out = [jnp.zeros((tok, 128), F32)] * active
    score_out = [jnp.zeros((tok, 128), F32)] * active
    for x_rel in range(2):
        for kk in range(ring):
            cols = slice(128 * (kk // 2), 128 * (kk // 2) + 128)
            turn = z - kk
            turn = jnp.where(turn < 0, turn + ring, turn)
            block = turn * 2 + (x ^ x_rel)
            pair = []
            for src in (code_src, score_src):
                near, far = src[x_rel][:, cols], src[2 + x_rel][:, cols]
                first = jnp.where(y == 0, near, far)
                second = jnp.where(y == 0, far, near)
                if kk % 2 == 0:
                    pair.append(jnp.where(low, first, pltpu.roll(second, 64, 1)))
                else:
                    pair.append(jnp.where(low, pltpu.roll(first, 64, 1), second))
            for k in range(active):
                hit = named[k] == block
                code_out[k] = code_out[k] + jnp.where(hit, pair[0], 0.0)
                score_out[k] = score_out[k] + jnp.where(hit, pair[1], 0.0)
    for k in range(active):
        out_codes[:, k, :] = code_out[k].astype(BF)
        out_scores[:, k, :] = score_out[k]


def move_weights(residual, gradient, block_ids, jump_mask, encoder, enc_bias, decoder, dec_bias):
    tok, width = residual.shape
    active = block_ids.shape[1]
    lanes = jump_mask.shape[2]
    lat_count = lax.axis_size("lat")
    ring = lat_count // 2
    per = lanes // 2
    half = width // 2
    names = ring * per

    def permute(values, to):
        pairs = []
        for gg in range(2):
            for ll in range(lat_count):
                for ss in range(2):
                    a, b, c = to(gg, ll, ss)
                    pairs.append(((gg * lat_count + ll) * 2 + ss, (a * lat_count + b) * 2 + c))
        return lax.ppermute(values, AXES, pairs)

    def by_x(v):
        return permute(v, lambda gg, ll, ss: (gg, ll ^ 1, ss))

    def by_y(v):
        return permute(v, lambda gg, ll, ss: (1 - gg, ll, ss))

    def by_xy(v):
        return permute(v, lambda gg, ll, ss: (1 - gg, ll ^ 1, ss))

    def by_core(v):
        return permute(v, lambda gg, ll, ss: (gg, ll, 1 - ss))

    def by_z(v, k):
        return permute(v, lambda gg, ll, ss: (gg, (ll + 2 * k) % lat_count, ss))

    (own,) = call(
        weights_kernel,
        [((per, 2 * half + 128), BF)],
        encoder, decoder, enc_bias.reshape(1, lanes),
        far=(0, 1),
        scratch=[pltpu.VMEM((half, lanes), BF), pltpu.SemaphoreType.DMA((2,))],
    )
    part_1 = by_z(own, 1)
    part_3 = by_z(own, -1)
    part_2 = by_z(part_1, 1)

    to_x, to_y, to_d, own_mask = call(
        functools.partial(tokens_kernel, ring),
        [((tok, 2 * width + names), BF)] * 3 + [((tok, names), BF)],
        residual, gradient, block_ids.T, jump_mask, own,
        far=(0, 1, 4),
        scratch=[pltpu.SemaphoreType.DMA((6,))],
    )
    own_rows = to_x
    rows, mask, recon, codes, scores, sums = call(
        early_kernel,
        [
            ((4 * tok, 2 * width), BF),
            ((4 * tok, names), BF),
            ((4 * tok, width), F32),
            ((4 * tok, names), BF),
            ((4 * tok, names), F32),
            ((8, names), F32),
        ],
        own_rows, own_mask, by_x(to_x), by_y(to_y), by_xy(to_d), encoder, decoder,
        own, part_1, by_core(part_1), part_3, by_core(part_3),
        far=(5, 6),
        scratch=[
            pltpu.VMEM((half, lanes), BF),
            pltpu.VMEM((per, 2 * half + 128), BF),
            pltpu.SemaphoreType.DMA((2,)),
        ],
    )
    own_recon, own_codes, own_scores, to_x, to_y, to_d, sums_2 = call(
        late_kernel,
        [((tok, width), F32), ((tok, names), BF), ((tok, names), F32)]
        + [((tok, width + 2 * names), BF)] * 3
        + [((8, 2 * per), F32)],
        rows, mask, recon, codes, scores, part_2, by_core(part_2),
    )
    from_d = by_xy(to_d)
    from_x = by_x(to_x)
    from_y = by_y(to_y)

    row, rest = call(
        functools.partial(totals_kernel, per),
        [((1, per), F32)] * 2,
        sums, by_z(sums, -1), by_z(sums_2, -2), by_z(sums, 1),
    )
    factor = (tok * lat_count * 2 * active / lat_count) ** (-0.5)
    latent_codes, attribution, recon_error, latent_totals = call(
        functools.partial(final_kernel, ring, factor),
        [
            ((tok, active, lanes), BF),
            ((tok, active, lanes), F32),
            ((tok, width), BF),
            ((1, per), F32),
        ],
        own_recon, own_codes, own_scores, from_x, from_y, from_d,
        own_rows, dec_bias.reshape(1, width), block_ids.T,
        permute(row, lambda gg, ll, ss: (ss, ll, gg)),
        permute(rest, lambda gg, ll, ss: (1 - ss, ll, gg)),
    )
    return (latent_codes, attribution, recon_error, latent_totals.reshape(per))


def solution(mesh):
    sizes = dict(mesh.shape)

    def on_device(residual, gradient, block_ids, jump_mask, encoder, enc_bias, decoder, dec_bias):
        lanes = jump_mask.shape[2]
        small = (
            sizes["groups"] == 2
            and sizes["seq"] == 2
            and sizes["lat"] == 8
            and encoder.shape[1] == lanes
            and lanes == 128
            and residual.shape[0] % 16 == 0
            and residual.shape[1] % 256 == 0
        )
        body = move_weights if small else move_tokens
        return body(
            residual, gradient, block_ids, jump_mask, encoder, enc_bias, decoder, dec_bias
        )

    rows = P(("groups", "lat", "seq"), None)
    cubes = P(("groups", "lat", "seq"), None, None)
    return jax.shard_map(
        on_device,
        mesh=mesh,
        in_specs=(rows, rows, rows, cubes, P(None, "lat"), P("lat"), P("lat", None), P()),
        out_specs=(cubes, cubes, rows, P(("groups", "lat", "seq"))),
        check_vma=False,
    )
```

```python
import functools

import jax
import jax.numpy as jnp
from jax import lax
from jax.experimental import pallas as pl
from jax.experimental.pallas import tpu as pltpu
from jax.sharding import PartitionSpec as P

AXES = ("groups", "lat", "seq")


def place_rows(values, source, filled, leading):
    picked = jnp.where(filled[:, None], values[source], jnp.zeros((), values.dtype))
    return picked.reshape(leading + (values.shape[-1],))


def move_tokens(residual, gradient, block_ids, jump_mask, encoder, enc_bias, decoder, dec_bias):
    tok_rows, width = residual.shape
    active = block_ids.shape[1]
    lanes = jump_mask.shape[2]
    lat_count = lax.axis_size("lat")
    seq_count = lax.axis_size("seq")
    local_blocks = encoder.shape[1] // lanes
    block_count = local_blocks * lat_count
    capacity = max(
        2, min(tok_rows, (3 * tok_rows * active + 2 * block_count - 1) // (2 * block_count))
    )
    slot_count = tok_rows * active
    flat_blocks = block_ids.reshape(slot_count)
    one_hot = (flat_blocks[:, None] == jnp.arange(block_count, dtype=jnp.int32)[None, :]).astype(
        jnp.int32
    )
    earlier = jnp.sum(jnp.cumsum(one_hot, axis=0) * one_hot, axis=1) - 1
    slot_id = flat_blocks * capacity + earlier
    owner_row = (
        jnp.zeros((block_count * capacity,), jnp.int32)
        .at[slot_id]
        .set(jnp.arange(slot_count, dtype=jnp.int32) + 1)
    )
    filled = owner_row > 0
    slot_source = jnp.maximum(owner_row - 1, 0)
    token_source = slot_source // active
    leading = (lat_count, local_blocks, capacity)
    enc_blocks = encoder.reshape(width, local_blocks, lanes)
    dec_blocks = decoder.reshape(local_blocks, lanes, width)
    bias_blocks = enc_bias.reshape(1, local_blocks, 1, lanes)
    mask_values = jump_mask.astype(jnp.float32)
    total_tokens = tok_rows * lat_count * seq_count
    factor = (total_tokens * active / block_count) ** (-0.5)

    def gather_home(slotted):
        last = slotted.shape[-1]
        return slotted.reshape(block_count * capacity, last)[slot_id].reshape(
            tok_rows, active, last
        )

    def swap(values):
        return lax.all_to_all(values, "lat", split_axis=0, concat_axis=0, tiled=True)

    residual_slots = place_rows(residual, token_source, filled, leading)
    gradient_slots = place_rows(gradient, token_source, filled, leading)
    preact = jnp.einsum(
        "sbcd,dbj->sbcj", swap(residual_slots), enc_blocks, preferred_element_type=jnp.float32
    )
    preact = swap((preact + bias_blocks).astype(jnp.bfloat16)).astype(jnp.float32)
    latent_codes = (gather_home(preact) * mask_values).astype(jnp.bfloat16)
    code_slots = place_rows(latent_codes.reshape(slot_count, lanes), slot_source, filled, leading)
    code_data = swap(code_slots)
    grad_data = swap(gradient_slots)
    score_data = code_data.astype(jnp.float32) * jnp.einsum(
        "sbcd,bjd->sbcj", grad_data, dec_blocks, preferred_element_type=jnp.float32
    )
    recon_data = jnp.einsum(
        "sbcj,bjd->sbcd", code_data, dec_blocks, preferred_element_type=jnp.float32
    )
    recon_home = gather_home(swap(recon_data.astype(jnp.bfloat16)))
    attribution = gather_home(swap(score_data))
    recon_error = (
        residual.astype(jnp.float32) - dec_bias - jnp.sum(recon_home.astype(jnp.float32), axis=1)
    ).astype(jnp.bfloat16)
    term = jnp.dot(
        one_hot.T.astype(jnp.float32),
        attribution.reshape(slot_count, lanes),
        precision=lax.Precision.HIGHEST,
    )
    latent_totals = (
        lax.psum_scatter(
            term.reshape(block_count * lanes), ("lat", "seq"), scatter_dimension=0, tiled=True
        )
        * factor
    )
    return (latent_codes, attribution, recon_error, latent_totals)


BF = jnp.bfloat16
F32 = jnp.float32


def nt(a, b):
    return lax.dot_general(a, b, (((1,), (1,)), ((), ())), preferred_element_type=F32)


def place_here():
    lat = lax.axis_index("lat")
    return lax.rem(lat, 2), lax.axis_index("groups"), lax.div(lat, 2), lax.axis_index("seq")


def call(kernel, outs, *args, far=(), scratch=(), vmem=24):
    return pl.pallas_call(
        kernel,
        in_specs=[
            pl.BlockSpec(memory_space=pl.ANY if i in far else pltpu.VMEM) for i in range(len(args))
        ],
        out_specs=[pl.BlockSpec(memory_space=pltpu.VMEM)] * len(outs),
        out_shape=[jax.ShapeDtypeStruct(*o) for o in outs],
        scratch_shapes=list(scratch),
        compiler_params=pltpu.CompilerParams(vmem_limit_bytes=vmem << 20),
    )(*args)


def pick_latents(per, lanes, y):
    row = lax.broadcasted_iota(jnp.int32, (per, lanes), 0)
    lane = lax.broadcasted_iota(jnp.int32, (per, lanes), 1)
    return (lane == row + per * y).astype(BF)


def weights_kernel(enc, dec, bias, out, enc_half, bias_here, sem):
    _, y, _, s = place_here()
    lanes = enc.shape[1]
    half = enc_half.shape[0]
    per = out.shape[0]
    chunks = 4
    n = half // chunks
    side = s * half
    copies = [pltpu.make_async_copy(bias, bias_here, sem.at[2 * chunks])]
    for i in range(chunks):
        copies.append(
            pltpu.make_async_copy(
                enc.at[pl.ds(pl.multiple_of(side + i * n, 64), n), :],
                enc_half.at[pl.ds(i * n, n), :],
                sem.at[i],
            )
        )
    m = per // chunks
    for i in range(chunks):
        copies.append(
            pltpu.make_async_copy(
                dec.at[
                    pl.ds(pl.multiple_of(y * per + i * m, 16), m),
                    pl.ds(pl.multiple_of(side, 128), half),
                ],
                out.at[pl.ds(i * m, m), pl.ds(half + 128, half)],
                sem.at[chunks + i],
            )
        )
    for copy in copies:
        copy.start()
    pick = pick_latents(per, lanes, y)
    copies[0].wait()
    b = bias_here[...]
    hi = b.astype(BF).astype(F32)
    mid = (b - hi).astype(BF).astype(F32)
    low = b - hi - mid
    term = lax.broadcasted_iota(jnp.int32, (lanes, lanes), 0)
    terms = jnp.where(term == 0, hi, jnp.where(term == 1, mid, jnp.where(term == 2, low, 0.0)))
    out[:, half : half + 128] = nt(pick, terms.astype(BF)).astype(BF)
    for copy in copies[1 : chunks + 1]:
        copy.wait()
    out[:, :half] = nt(pick, enc_half[...]).astype(BF)
    for copy in copies[chunks + 1 :]:
        copy.wait()


def totals_kernel(early, two, three, row, rest):
    _, y, _, s = place_here()
    per = row.shape[1]
    total = early[:2] + two[:2] + pltpu.roll(three[...], per, 1)[:2]
    row[...] = jnp.where(y == s, total[:1, :per], total[1:, :per])
    rest[...] = jnp.where(y == s, total[1:, :per], total[:1, :per])


def after_kernel(values, _, out):
    out[...] = values[...]


def target_block(lane, m, x, z, ring):
    turn = z - 2 * m - (lane >= 64).astype(jnp.int32)
    turn = jnp.where(turn < 0, turn + ring, turn)
    return turn * 2 + x


def tokens_kernel(ring, res, grad, ids, jump, _, to_x, to_y, to_d, own_mask, sem):
    x, y, z, _ = place_here()
    tok, width = res.shape
    active = ids.shape[0]
    outs = (to_x, to_y, to_d)
    copies = []
    for i, src in enumerate((res, grad)):
        for j, out in enumerate(outs):
            copies.append(
                pltpu.make_async_copy(src, out.at[:, pl.ds(i * width, width)], sem.at[3 * i + j])
            )
    for copy in copies:
        copy.start()
    names = ids[...].T
    names = [jnp.broadcast_to(names[:, k : k + 1], (tok, 128)) for k in range(active)]
    lane = lax.broadcasted_iota(jnp.int32, (tok, 128), 1)
    low = lane < 64
    plain = [jump[:, k, :] for k in range(active)]
    moved = [pltpu.roll(v, 64, 1) for v in plain]
    for dest in range(4):
        x_rel, y_rel = dest % 2, dest // 2
        first = (y ^ y_rel) == 0
        for m in range(ring // 2):
            tgt = target_block(lane, m, x ^ x_rel, z, ring)
            total = jnp.zeros((tok, 128), jnp.int32)
            for k in range(active):
                value = jnp.where(low == first, plain[k], moved[k])
                total = total + jnp.where(names[k] == tgt, value, 0)
            out = total.astype(F32).astype(BF)
            if dest == 0:
                own_mask[:, m * 128 : m * 128 + 128] = out
            else:
                at = 2 * width + m * 128
                outs[dest - 1][:, at : at + 128] = out
    for copy in copies:
        copy.wait()


def group_sums(scores):
    half = scores.shape[0] // 2
    near = jnp.sum(scores[:half], axis=0, keepdims=True)
    far = jnp.sum(scores[half:], axis=0, keepdims=True)
    return jnp.concatenate([near, far, jnp.zeros((6, scores.shape[1]), F32)], axis=0)


def blocks(rows, mask, sides, half):
    bias = jnp.concatenate([p[:, half : half + 128] for p in sides[0]], axis=0)
    preact = nt(jnp.ones((8, 128), BF), bias)[:1]
    for j, parts in enumerate(sides):
        weights = jnp.concatenate([p[:, :half] for p in parts], axis=0)
        preact = preact + nt(rows[:, j * half : (j + 1) * half], weights)
    code = (preact * mask.astype(F32)).astype(BF)
    proj = jnp.zeros(code.shape, F32)
    recon = []
    for j, parts in enumerate(sides):
        weights = jnp.concatenate([p[:, half + 128 :] for p in parts], axis=0)
        proj = proj + nt(rows[:, (2 + j) * half : (3 + j) * half], weights)
        recon.append(jnp.dot(code, weights, preferred_element_type=F32))
    return code, code.astype(F32) * proj, recon


def early_kernel(
    from_d, from_x, from_y, own, own_mask, enc, dec, mine_0, mine_1, other_1,
    rows, mask, recon, codes, scores, sums, enc_half, other_0, sem,
):
    _, y, _, s = place_here()
    tok = own.shape[0]
    per, lanes = other_0.shape[0], enc.shape[1]
    half = enc_half.shape[0]
    width = 2 * half
    far = pl.ds(pl.multiple_of((1 - s) * half, 128), half)
    get_enc = pltpu.make_async_copy(enc.at[far, :], enc_half, sem.at[0])
    get_dec = pltpu.make_async_copy(
        dec.at[pl.ds(pl.multiple_of(y * per, 16), per), far],
        other_0.at[:, pl.ds(half + 128, half)],
        sem.at[1],
    )
    get_enc.start()
    get_dec.start()
    for i, src in enumerate((own, from_x, from_y, from_d)):
        at = slice(i * tok, (i + 1) * tok)
        mask[at] = own_mask[...] if i == 0 else src[:, 2 * width :]
        for j in range(4):
            side = s if j % 2 == 0 else 1 - s
            cols = pl.ds(pl.multiple_of(width * (j // 2) + side * half, 128), half)
            rows[at, j * half : (j + 1) * half] = src[:, cols]
    other_0[:, half : half + 128] = jnp.zeros((per, 128), BF)
    get_enc.wait()
    other_0[:, :half] = nt(pick_latents(per, lanes, y), enc_half[...]).astype(BF)
    get_dec.wait()
    code, score, total = blocks(
        rows, mask[:, : 2 * per], ((mine_0, mine_1), (other_0, other_1)), half
    )
    codes[...] = code
    scores[...] = score
    for j in range(2):
        recon[:, j * half : (j + 1) * half] = total[j]
    sums[...] = group_sums(score)


def late_kernel(
    rows, mask, recon, codes, scores, mine_2, other_2, mine_3, other_3, sums, one,
    own_recon, own_codes, own_scores, to_x, to_y, to_d, sums_23, sums_01,
):
    _, _, _, s = place_here()
    per = mine_2.shape[0]
    tok = own_codes.shape[0]
    width = own_recon.shape[1]
    half = width // 2
    code, score, total = blocks(
        rows, mask[:, 2 * per :], ((mine_2, mine_3), (other_2, other_3)), half
    )
    for j in range(2):
        cols = pl.ds(pl.multiple_of((s if j == 0 else 1 - s) * half, 128), half)
        part = recon[:, j * half : (j + 1) * half] + total[j]
        for i, out in enumerate((own_recon, to_x, to_y, to_d)):
            out[:, cols] = part[i * tok : (i + 1) * tok].astype(out.dtype)
    sums_23[...] = group_sums(score)
    sums_01[...] = sums[...] + pltpu.roll(one[...], per, 1)
    own_codes[...] = jnp.concatenate([codes[:tok], code[:tok]], axis=1)
    own_scores[...] = jnp.concatenate([scores[:tok], score[:tok]], axis=1)
    for i, out in enumerate((to_x, to_y, to_d)):
        at = slice((i + 1) * tok, (i + 2) * tok)
        for j, (first, second) in enumerate(((codes, code), (scores, score))):
            base = width + 4 * per * j
            out[:, base : base + 2 * per] = first[at].astype(BF)
            out[:, base + 2 * per : base + 4 * per] = second[at].astype(BF)


def final_kernel(
    ring, factor, from_d, from_x, from_y, own_recon, own_codes, own_scores, own, dec_bias, ids, row, rest,
    out_codes, out_scores, out_error, out_totals,
):
    x, y, z, _ = place_here()
    out_totals[...] = (row[...] + rest[...]) * factor
    tok, width = own_recon.shape
    names = own_codes.shape[1]
    active = ids.shape[0]
    named = ids[...].T
    named = [jnp.broadcast_to(named[:, k : k + 1], (tok, 128)) for k in range(active)]
    others = (from_x, from_y, from_d)
    recon = own_recon[...]
    for src in others:
        recon = recon + src[:, :width].astype(F32)
    out_error[...] = (own[:, :width].astype(F32) - dec_bias[...] - recon).astype(BF)
    code_src = [own_codes[...].astype(F32)]
    score_src = [own_scores[...]]
    for src in others:
        code_src.append(src[:, width : width + names].astype(F32))
        score_src.append(src[:, width + names :].astype(F32))
    lane = lax.broadcasted_iota(jnp.int32, (tok, 128), 1)
    low = lane < 64
    code_out = [jnp.zeros((tok, 128), F32)] * active
    score_out = [jnp.zeros((tok, 128), F32)] * active
    for x_rel in range(2):
        for kk in range(ring):
            cols = slice(128 * (kk // 2), 128 * (kk // 2) + 128)
            turn = z - kk
            turn = jnp.where(turn < 0, turn + ring, turn)
            block = turn * 2 + (x ^ x_rel)
            pair = []
            for src in (code_src, score_src):
                near, far = src[x_rel][:, cols], src[2 + x_rel][:, cols]
                first = jnp.where(y == 0, near, far)
                second = jnp.where(y == 0, far, near)
                if kk % 2 == 0:
                    pair.append(jnp.where(low, first, pltpu.roll(second, 64, 1)))
                else:
                    pair.append(jnp.where(low, pltpu.roll(first, 64, 1), second))
            for k in range(active):
                hit = named[k] == block
                code_out[k] = code_out[k] + jnp.where(hit, pair[0], 0.0)
                score_out[k] = score_out[k] + jnp.where(hit, pair[1], 0.0)
    for k in range(active):
        out_codes[:, k, :] = code_out[k].astype(BF)
        out_scores[:, k, :] = score_out[k]


def move_weights(residual, gradient, block_ids, jump_mask, encoder, enc_bias, decoder, dec_bias):
    tok, width = residual.shape
    active = block_ids.shape[1]
    lanes = jump_mask.shape[2]
    lat_count = lax.axis_size("lat")
    ring = lat_count // 2
    per = lanes // 2
    half = width // 2
    names = ring * per

    def permute(values, to):
        pairs = []
        for gg in range(2):
            for ll in range(lat_count):
                for ss in range(2):
                    a, b, c = to(gg, ll, ss)
                    pairs.append(((gg * lat_count + ll) * 2 + ss, (a * lat_count + b) * 2 + c))
        return lax.ppermute(values, AXES, pairs)

    def by_x(v):
        return permute(v, lambda gg, ll, ss: (gg, ll ^ 1, ss))

    def by_y(v):
        return permute(v, lambda gg, ll, ss: (1 - gg, ll, ss))

    def by_xy(v):
        return permute(v, lambda gg, ll, ss: (1 - gg, ll ^ 1, ss))

    def by_core(v):
        return permute(v, lambda gg, ll, ss: (gg, ll, 1 - ss))

    def by_z(v, k):
        return permute(v, lambda gg, ll, ss: (gg, (ll + 2 * k) % lat_count, ss))

    (own,) = call(
        weights_kernel,
        [((per, 2 * half + 128), BF)],
        encoder, decoder, enc_bias.reshape(1, lanes),
        far=(0, 1, 2),
        scratch=[
            pltpu.VMEM((half, lanes), BF),
            pltpu.VMEM((1, lanes), F32),
            pltpu.SemaphoreType.DMA((9,)),
        ],
        vmem=56,
    )
    part_1 = by_z(own, 1)
    part_2 = by_z(part_1, 1)
    part_3 = by_z(own, -1)

    to_x, to_y, to_d, own_mask = call(
        functools.partial(tokens_kernel, ring),
        [((tok, 2 * width + names), BF)] * 3 + [((tok, names), BF)],
        residual, gradient, block_ids.T, jump_mask, own,
        far=(0, 1, 4),
        scratch=[pltpu.SemaphoreType.DMA((6,))],
    )
    own_rows = to_d
    from_d = by_xy(to_d)
    from_x = by_x(to_x)
    from_y = by_y(to_y)
    rows, mask, recon, codes, scores, sums = call(
        early_kernel,
        [
            ((4 * tok, 2 * width), BF),
            ((4 * tok, names), BF),
            ((4 * tok, width), F32),
            ((4 * tok, 2 * per), BF),
            ((4 * tok, 2 * per), F32),
            ((8, 2 * per), F32),
        ],
        from_d, from_x, from_y, own_rows, own_mask, encoder, decoder,
        own, part_1, by_core(part_1),
        far=(5, 6),
        scratch=[
            pltpu.VMEM((half, lanes), BF),
            pltpu.VMEM((per, 2 * half + 128), BF),
            pltpu.SemaphoreType.DMA((2,)),
        ],
    )
    (part_2,) = call(after_kernel, [(part_2.shape, BF)], part_2, codes, far=(1,))
    own_recon, own_codes, own_scores, to_x, to_y, to_d, sums_23, sums_01 = call(
        late_kernel,
        [((tok, width), F32), ((tok, names), BF), ((tok, names), F32)]
        + [((tok, width + 2 * names), BF)] * 3
        + [((8, 2 * per), F32)] * 2,
        rows, mask, recon, codes, scores, part_2, by_core(part_2), part_3, by_core(part_3),
        sums, by_z(sums, -1),
    )
    from_d = by_xy(to_d)
    from_x = by_x(to_x)
    from_y = by_y(to_y)

    row, rest = call(
        totals_kernel,
        [((1, per), F32)] * 2,
        sums_01, by_z(sums_23, -2), by_z(sums_23, 1),
    )
    factor = (tok * lat_count * 2 * active / lat_count) ** (-0.5)
    latent_codes, attribution, recon_error, latent_totals = call(
        functools.partial(final_kernel, ring, factor),
        [
            ((tok, active, lanes), BF),
            ((tok, active, lanes), F32),
            ((tok, width), BF),
            ((1, per), F32),
        ],
        from_d, from_x, from_y, own_recon, own_codes, own_scores,
        own_rows, dec_bias.reshape(1, width), block_ids.T,
        permute(row, lambda gg, ll, ss: (ss, ll, gg)),
        permute(rest, lambda gg, ll, ss: (1 - ss, ll, gg)),
    )
    return (latent_codes, attribution, recon_error, latent_totals.reshape(per))


def solution(mesh):
    sizes = dict(mesh.shape)

    def on_device(residual, gradient, block_ids, jump_mask, encoder, enc_bias, decoder, dec_bias):
        lanes = jump_mask.shape[2]
        small = (
            sizes["groups"] == 2
            and sizes["seq"] == 2
            and sizes["lat"] == 8
            and encoder.shape[1] == lanes
            and lanes == 128
            and residual.shape[0] % 16 == 0
            and residual.shape[1] % 256 == 0
        )
        body = move_weights if small else move_tokens
        return body(
            residual, gradient, block_ids, jump_mask, encoder, enc_bias, decoder, dec_bias
        )

    rows = P(("groups", "lat", "seq"), None)
    cubes = P(("groups", "lat", "seq"), None, None)
    return jax.shard_map(
        on_device,
        mesh=mesh,
        in_specs=(rows, rows, rows, cubes, P(None, "lat"), P("lat"), P("lat", None), P()),
        out_specs=(cubes, cubes, rows, P(("groups", "lat", "seq"))),
        check_vma=False,
    )
```

```python
import functools

import jax
import jax.numpy as jnp
from jax import lax
from jax.experimental import pallas as pl
from jax.experimental.pallas import tpu as pltpu
from jax.sharding import PartitionSpec as P

AXES = ("groups", "lat", "seq")


def place_rows(values, source, filled, leading):
    picked = jnp.where(filled[:, None], values[source], jnp.zeros((), values.dtype))
    return picked.reshape(leading + (values.shape[-1],))


def move_tokens(residual, gradient, block_ids, jump_mask, encoder, enc_bias, decoder, dec_bias):
    tok_rows, width = residual.shape
    active = block_ids.shape[1]
    lanes = jump_mask.shape[2]
    lat_count = lax.axis_size("lat")
    seq_count = lax.axis_size("seq")
    local_blocks = encoder.shape[1] // lanes
    block_count = local_blocks * lat_count
    capacity = max(
        2, min(tok_rows, (3 * tok_rows * active + 2 * block_count - 1) // (2 * block_count))
    )
    slot_count = tok_rows * active
    flat_blocks = block_ids.reshape(slot_count)
    one_hot = (flat_blocks[:, None] == jnp.arange(block_count, dtype=jnp.int32)[None, :]).astype(
        jnp.int32
    )
    earlier = jnp.sum(jnp.cumsum(one_hot, axis=0) * one_hot, axis=1) - 1
    slot_id = flat_blocks * capacity + earlier
    owner_row = (
        jnp.zeros((block_count * capacity,), jnp.int32)
        .at[slot_id]
        .set(jnp.arange(slot_count, dtype=jnp.int32) + 1)
    )
    filled = owner_row > 0
    slot_source = jnp.maximum(owner_row - 1, 0)
    token_source = slot_source // active
    leading = (lat_count, local_blocks, capacity)
    enc_blocks = encoder.reshape(width, local_blocks, lanes)
    dec_blocks = decoder.reshape(local_blocks, lanes, width)
    bias_blocks = enc_bias.reshape(1, local_blocks, 1, lanes)
    mask_values = jump_mask.astype(jnp.float32)
    total_tokens = tok_rows * lat_count * seq_count
    factor = (total_tokens * active / block_count) ** (-0.5)

    def gather_home(slotted):
        last = slotted.shape[-1]
        return slotted.reshape(block_count * capacity, last)[slot_id].reshape(
            tok_rows, active, last
        )

    def swap(values):
        return lax.all_to_all(values, "lat", split_axis=0, concat_axis=0, tiled=True)

    residual_slots = place_rows(residual, token_source, filled, leading)
    gradient_slots = place_rows(gradient, token_source, filled, leading)
    preact = jnp.einsum(
        "sbcd,dbj->sbcj", swap(residual_slots), enc_blocks, preferred_element_type=jnp.float32
    )
    preact = swap((preact + bias_blocks).astype(jnp.bfloat16)).astype(jnp.float32)
    latent_codes = (gather_home(preact) * mask_values).astype(jnp.bfloat16)
    code_slots = place_rows(latent_codes.reshape(slot_count, lanes), slot_source, filled, leading)
    code_data = swap(code_slots)
    grad_data = swap(gradient_slots)
    score_data = code_data.astype(jnp.float32) * jnp.einsum(
        "sbcd,bjd->sbcj", grad_data, dec_blocks, preferred_element_type=jnp.float32
    )
    recon_data = jnp.einsum(
        "sbcj,bjd->sbcd", code_data, dec_blocks, preferred_element_type=jnp.float32
    )
    recon_home = gather_home(swap(recon_data.astype(jnp.bfloat16)))
    attribution = gather_home(swap(score_data))
    recon_error = (
        residual.astype(jnp.float32) - dec_bias - jnp.sum(recon_home.astype(jnp.float32), axis=1)
    ).astype(jnp.bfloat16)
    term = jnp.dot(
        one_hot.T.astype(jnp.float32),
        attribution.reshape(slot_count, lanes),
        precision=lax.Precision.HIGHEST,
    )
    latent_totals = (
        lax.psum_scatter(
            term.reshape(block_count * lanes), ("lat", "seq"), scatter_dimension=0, tiled=True
        )
        * factor
    )
    return (latent_codes, attribution, recon_error, latent_totals)


BF = jnp.bfloat16
F32 = jnp.float32


def nt(a, b):
    return lax.dot_general(a, b, (((1,), (1,)), ((), ())), preferred_element_type=F32)


def place_here():
    lat = lax.axis_index("lat")
    return lax.rem(lat, 2), lax.axis_index("groups"), lax.div(lat, 2), lax.axis_index("seq")


def call(kernel, outs, *args, far=(), scratch=(), vmem=24):
    return pl.pallas_call(
        kernel,
        in_specs=[
            pl.BlockSpec(memory_space=pl.ANY if i in far else pltpu.VMEM) for i in range(len(args))
        ],
        out_specs=[pl.BlockSpec(memory_space=pltpu.VMEM)] * len(outs),
        out_shape=[jax.ShapeDtypeStruct(*o) for o in outs],
        scratch_shapes=list(scratch),
        compiler_params=pltpu.CompilerParams(vmem_limit_bytes=vmem << 20),
    )(*args)


def pick_latents(per, lanes, y):
    row = lax.broadcasted_iota(jnp.int32, (per, lanes), 0)
    lane = lax.broadcasted_iota(jnp.int32, (per, lanes), 1)
    return (lane == row + per * y).astype(BF)


def weights_kernel(enc, dec, bias, out, enc_half, bias_here, sem):
    _, y, _, s = place_here()
    lanes = enc.shape[1]
    half = enc_half.shape[0]
    per = out.shape[0]
    chunks = 4
    n = half // chunks
    side = s * half
    copies = [pltpu.make_async_copy(bias, bias_here, sem.at[2 * chunks])]
    for i in range(chunks):
        copies.append(
            pltpu.make_async_copy(
                enc.at[pl.ds(pl.multiple_of(side + i * n, 64), n), :],
                enc_half.at[pl.ds(i * n, n), :],
                sem.at[i],
            )
        )
    m = per // chunks
    for i in range(chunks):
        copies.append(
            pltpu.make_async_copy(
                dec.at[
                    pl.ds(pl.multiple_of(y * per + i * m, 16), m),
                    pl.ds(pl.multiple_of(side, 128), half),
                ],
                out.at[pl.ds(i * m, m), pl.ds(half + 128, half)],
                sem.at[chunks + i],
            )
        )
    for copy in copies:
        copy.start()
    pick = pick_latents(per, lanes, y)
    copies[0].wait()
    b = bias_here[...]
    hi = b.astype(BF).astype(F32)
    mid = (b - hi).astype(BF).astype(F32)
    low = b - hi - mid
    term = lax.broadcasted_iota(jnp.int32, (lanes, lanes), 0)
    terms = jnp.where(term == 0, hi, jnp.where(term == 1, mid, jnp.where(term == 2, low, 0.0)))
    out[:, half : half + 128] = nt(pick, terms.astype(BF)).astype(BF)
    for copy in copies[1 : chunks + 1]:
        copy.wait()
    out[:, :half] = nt(pick, enc_half[...]).astype(BF)
    for copy in copies[chunks + 1 :]:
        copy.wait()


def totals_kernel(early, two, three, row, rest):
    _, y, _, s = place_here()
    per = row.shape[1]
    total = early[:2] + two[:2] + pltpu.roll(three[...], per, 1)[:2]
    row[...] = jnp.where(y == s, total[:1, :per], total[1:, :per])
    rest[...] = jnp.where(y == s, total[1:, :per], total[:1, :per])


def after_kernel(*refs):
    del refs


def target_block(lane, m, x, z, ring):
    turn = z - 2 * m - (lane >= 64).astype(jnp.int32)
    turn = jnp.where(turn < 0, turn + ring, turn)
    return turn * 2 + x


def tokens_kernel(ring, res, grad, ids, jump, _, to_x, to_y, to_d, own_mask, sem):
    x, y, z, _ = place_here()
    tok, width = res.shape
    active = ids.shape[0]
    outs = (to_x, to_y, to_d)
    copies = []
    for i, src in enumerate((res, grad)):
        for j, out in enumerate(outs):
            copies.append(
                pltpu.make_async_copy(src, out.at[:, pl.ds(i * width, width)], sem.at[3 * i + j])
            )
    for copy in copies:
        copy.start()
    names = ids[...].T
    names = [jnp.broadcast_to(names[:, k : k + 1], (tok, 128)) for k in range(active)]
    lane = lax.broadcasted_iota(jnp.int32, (tok, 128), 1)
    low = lane < 64
    plain = [jump[:, k, :] for k in range(active)]
    moved = [pltpu.roll(v, 64, 1) for v in plain]
    for dest in range(4):
        x_rel, y_rel = dest % 2, dest // 2
        first = (y ^ y_rel) == 0
        for m in range(ring // 2):
            tgt = target_block(lane, m, x ^ x_rel, z, ring)
            total = jnp.zeros((tok, 128), jnp.int32)
            for k in range(active):
                value = jnp.where(low == first, plain[k], moved[k])
                total = total + jnp.where(names[k] == tgt, value, 0)
            out = total.astype(F32).astype(BF)
            if dest == 0:
                own_mask[:, m * 128 : m * 128 + 128] = out
            else:
                at = 2 * width + m * 128
                outs[dest - 1][:, at : at + 128] = out
    for copy in copies:
        copy.wait()


def group_sums(scores):
    half = scores.shape[0] // 2
    near = jnp.sum(scores[:half], axis=0, keepdims=True)
    far = jnp.sum(scores[half:], axis=0, keepdims=True)
    return jnp.concatenate([near, far, jnp.zeros((6, scores.shape[1]), F32)], axis=0)


def blocks(rows, mask, sides, half):
    bias = jnp.concatenate([p[:, half : half + 128] for p in sides[0]], axis=0)
    preact = nt(jnp.ones((8, 128), BF), bias)[:1]
    for j, parts in enumerate(sides):
        weights = jnp.concatenate([p[:, :half] for p in parts], axis=0)
        preact = preact + nt(rows[:, j * half : (j + 1) * half], weights)
    code = (preact * mask.astype(F32)).astype(BF)
    proj = jnp.zeros(code.shape, F32)
    recon = []
    for j, parts in enumerate(sides):
        weights = jnp.concatenate([p[:, half + 128 :] for p in parts], axis=0)
        proj = proj + nt(rows[:, (2 + j) * half : (3 + j) * half], weights)
        recon.append(jnp.dot(code, weights, preferred_element_type=F32))
    return code, code.astype(F32) * proj, recon


def early_kernel(
    from_d, from_x, from_y, own, own_mask, enc, dec, mine_0, mine_1, other_1,
    rows, mask, recon, codes, scores, sums, enc_half, other_0, sem,
):
    _, y, _, s = place_here()
    tok = own.shape[0]
    per, lanes = other_0.shape[0], enc.shape[1]
    half = enc_half.shape[0]
    width = 2 * half
    far = pl.ds(pl.multiple_of((1 - s) * half, 128), half)
    get_enc = pltpu.make_async_copy(enc.at[far, :], enc_half, sem.at[0])
    get_dec = pltpu.make_async_copy(
        dec.at[pl.ds(pl.multiple_of(y * per, 16), per), far],
        other_0.at[:, pl.ds(half + 128, half)],
        sem.at[1],
    )
    get_enc.start()
    get_dec.start()
    for i, src in enumerate((own, from_x, from_y, from_d)):
        at = slice(i * tok, (i + 1) * tok)
        mask[at] = own_mask[...] if i == 0 else src[:, 2 * width :]
        for j in range(4):
            side = s if j % 2 == 0 else 1 - s
            cols = pl.ds(pl.multiple_of(width * (j // 2) + side * half, 128), half)
            rows[at, j * half : (j + 1) * half] = src[:, cols]
    other_0[:, half : half + 128] = jnp.zeros((per, 128), BF)
    get_enc.wait()
    other_0[:, :half] = nt(pick_latents(per, lanes, y), enc_half[...]).astype(BF)
    get_dec.wait()
    code, score, total = blocks(
        rows, mask[:, : 2 * per], ((mine_0, mine_1), (other_0, other_1)), half
    )
    codes[...] = code
    scores[...] = score
    for j in range(2):
        recon[:, j * half : (j + 1) * half] = total[j]
    sums[...] = group_sums(score)


def late_kernel(
    rows, mask, recon, codes, scores, mine_2, other_2, mine_3, other_3, sums, one,
    own_recon, own_codes, own_scores, to_x, to_y, to_d, sums_23, sums_01,
):
    _, _, _, s = place_here()
    per = mine_2.shape[0]
    tok = own_codes.shape[0]
    width = own_recon.shape[1]
    half = width // 2
    code, score, total = blocks(
        rows, mask[:, 2 * per :], ((mine_2, mine_3), (other_2, other_3)), half
    )
    for j in range(2):
        cols = pl.ds(pl.multiple_of((s if j == 0 else 1 - s) * half, 128), half)
        part = recon[:, j * half : (j + 1) * half] + total[j]
        for i, out in enumerate((own_recon, to_x, to_y, to_d)):
            out[:, cols] = part[i * tok : (i + 1) * tok].astype(out.dtype)
    sums_23[...] = group_sums(score)
    sums_01[...] = sums[...] + pltpu.roll(one[...], per, 1)
    own_codes[...] = jnp.concatenate([codes[:tok], code[:tok]], axis=1)
    own_scores[...] = jnp.concatenate([scores[:tok], score[:tok]], axis=1)
    for i, out in enumerate((to_x, to_y, to_d)):
        at = slice((i + 1) * tok, (i + 2) * tok)
        for j, (first, second) in enumerate(((codes, code), (scores, score))):
            base = width + 4 * per * j
            out[:, base : base + 2 * per] = first[at].astype(BF)
            out[:, base + 2 * per : base + 4 * per] = second[at].astype(BF)


def final_kernel(
    ring, factor, from_d, from_x, from_y, own_recon, own_codes, own_scores, own, dec_bias, ids, row, rest,
    out_codes, out_scores, out_error, out_totals,
):
    x, y, z, _ = place_here()
    out_totals[...] = (row[...] + rest[...]) * factor
    tok, width = own_recon.shape
    names = own_codes.shape[1]
    active = ids.shape[0]
    named = ids[...].T
    named = [jnp.broadcast_to(named[:, k : k + 1], (tok, 128)) for k in range(active)]
    others = (from_x, from_y, from_d)
    recon = own_recon[...]
    for src in others:
        recon = recon + src[:, :width].astype(F32)
    out_error[...] = (own[:, :width].astype(F32) - dec_bias[...] - recon).astype(BF)
    code_src = [own_codes[...].astype(F32)]
    score_src = [own_scores[...]]
    for src in others:
        code_src.append(src[:, width : width + names].astype(F32))
        score_src.append(src[:, width + names :].astype(F32))
    lane = lax.broadcasted_iota(jnp.int32, (tok, 128), 1)
    low = lane < 64
    code_out = [jnp.zeros((tok, 128), F32)] * active
    score_out = [jnp.zeros((tok, 128), F32)] * active
    for x_rel in range(2):
        for kk in range(ring):
            cols = slice(128 * (kk // 2), 128 * (kk // 2) + 128)
            turn = z - kk
            turn = jnp.where(turn < 0, turn + ring, turn)
            block = turn * 2 + (x ^ x_rel)
            pair = []
            for src in (code_src, score_src):
                near, far = src[x_rel][:, cols], src[2 + x_rel][:, cols]
                first = jnp.where(y == 0, near, far)
                second = jnp.where(y == 0, far, near)
                if kk % 2 == 0:
                    pair.append(jnp.where(low, first, pltpu.roll(second, 64, 1)))
                else:
                    pair.append(jnp.where(low, pltpu.roll(first, 64, 1), second))
            for k in range(active):
                hit = named[k] == block
                code_out[k] = code_out[k] + jnp.where(hit, pair[0], 0.0)
                score_out[k] = score_out[k] + jnp.where(hit, pair[1], 0.0)
    for k in range(active):
        out_codes[:, k, :] = code_out[k].astype(BF)
        out_scores[:, k, :] = score_out[k]


def move_weights(residual, gradient, block_ids, jump_mask, encoder, enc_bias, decoder, dec_bias):
    tok, width = residual.shape
    active = block_ids.shape[1]
    lanes = jump_mask.shape[2]
    lat_count = lax.axis_size("lat")
    ring = lat_count // 2
    per = lanes // 2
    half = width // 2
    names = ring * per

    def permute(values, to):
        pairs = []
        for gg in range(2):
            for ll in range(lat_count):
                for ss in range(2):
                    a, b, c = to(gg, ll, ss)
                    pairs.append(((gg * lat_count + ll) * 2 + ss, (a * lat_count + b) * 2 + c))
        return lax.ppermute(values, AXES, pairs)

    def by_x(v):
        return permute(v, lambda gg, ll, ss: (gg, ll ^ 1, ss))

    def by_y(v):
        return permute(v, lambda gg, ll, ss: (1 - gg, ll, ss))

    def by_xy(v):
        return permute(v, lambda gg, ll, ss: (1 - gg, ll ^ 1, ss))

    def by_core(v):
        return permute(v, lambda gg, ll, ss: (gg, ll, 1 - ss))

    def by_z(v, k):
        return permute(v, lambda gg, ll, ss: (gg, (ll + 2 * k) % lat_count, ss))

    (own,) = call(
        weights_kernel,
        [((per, 2 * half + 128), BF)],
        encoder, decoder, enc_bias.reshape(1, lanes),
        far=(0, 1, 2),
        scratch=[
            pltpu.VMEM((half, lanes), BF),
            pltpu.VMEM((1, lanes), F32),
            pltpu.SemaphoreType.DMA((9,)),
        ],
        vmem=56,
    )
    part_1 = by_z(own, 1)
    part_2 = by_z(part_1, 1)
    part_3 = by_z(own, -1)

    to_x, to_y, to_d, own_mask = call(
        functools.partial(tokens_kernel, ring),
        [((tok, 2 * width + names), BF)] * 3 + [((tok, names), BF)],
        residual, gradient, block_ids.T, jump_mask, own,
        far=(0, 1, 4),
        scratch=[pltpu.SemaphoreType.DMA((6,))],
    )
    own_rows = to_d
    from_d = by_xy(to_d)
    from_x = by_x(to_x)
    from_y = by_y(to_y)
    rows, mask, recon, codes, scores, sums = call(
        early_kernel,
        [
            ((4 * tok, 2 * width), BF),
            ((4 * tok, names), BF),
            ((4 * tok, width), F32),
            ((4 * tok, 2 * per), BF),
            ((4 * tok, 2 * per), F32),
            ((8, 2 * per), F32),
        ],
        from_d, from_x, from_y, own_rows, own_mask, encoder, decoder,
        own, part_1, by_core(part_1),
        far=(5, 6),
        scratch=[
            pltpu.VMEM((half, lanes), BF),
            pltpu.VMEM((per, 2 * half + 128), BF),
            pltpu.SemaphoreType.DMA((2,)),
        ],
    )
    part_2 = pl.pallas_call(
        after_kernel,
        in_specs=[pl.BlockSpec(memory_space=pl.ANY)] * 2,
        out_specs=pl.BlockSpec(memory_space=pl.ANY),
        out_shape=jax.ShapeDtypeStruct(part_2.shape, BF),
        input_output_aliases={0: 0},
        compiler_params=pltpu.CompilerParams(vmem_limit_bytes=1 << 20),
    )(part_2, codes)
    own_recon, own_codes, own_scores, to_x, to_y, to_d, sums_23, sums_01 = call(
        late_kernel,
        [((tok, width), F32), ((tok, names), BF), ((tok, names), F32)]
        + [((tok, width + 2 * names), BF)] * 3
        + [((8, 2 * per), F32)] * 2,
        rows, mask, recon, codes, scores, part_2, by_core(part_2), part_3, by_core(part_3),
        sums, by_z(sums, -1),
    )
    from_d = by_xy(to_d)
    from_x = by_x(to_x)
    from_y = by_y(to_y)

    row, rest = call(
        totals_kernel,
        [((1, per), F32)] * 2,
        sums_01, by_z(sums_23, -2), by_z(sums_23, 1),
    )
    factor = (tok * lat_count * 2 * active / lat_count) ** (-0.5)
    latent_codes, attribution, recon_error, latent_totals = call(
        functools.partial(final_kernel, ring, factor),
        [
            ((tok, active, lanes), BF),
            ((tok, active, lanes), F32),
            ((tok, width), BF),
            ((1, per), F32),
        ],
        from_d, from_x, from_y, own_recon, own_codes, own_scores,
        own_rows, dec_bias.reshape(1, width), block_ids.T,
        permute(row, lambda gg, ll, ss: (ss, ll, gg)),
        permute(rest, lambda gg, ll, ss: (1 - ss, ll, gg)),
    )
    return (latent_codes, attribution, recon_error, latent_totals.reshape(per))


def solution(mesh):
    sizes = dict(mesh.shape)

    def on_device(residual, gradient, block_ids, jump_mask, encoder, enc_bias, decoder, dec_bias):
        lanes = jump_mask.shape[2]
        small = (
            sizes["groups"] == 2
            and sizes["seq"] == 2
            and sizes["lat"] == 8
            and encoder.shape[1] == lanes
            and lanes == 128
            and residual.shape[0] % 16 == 0
            and residual.shape[1] % 256 == 0
        )
        body = move_weights if small else move_tokens
        return body(
            residual, gradient, block_ids, jump_mask, encoder, enc_bias, decoder, dec_bias
        )

    rows = P(("groups", "lat", "seq"), None)
    cubes = P(("groups", "lat", "seq"), None, None)
    return jax.shard_map(
        on_device,
        mesh=mesh,
        in_specs=(rows, rows, rows, cubes, P(None, "lat"), P("lat"), P("lat", None), P()),
        out_specs=(cubes, cubes, rows, P(("groups", "lat", "seq"))),
        check_vma=False,
    )
```

```python
import functools

import jax
import jax.numpy as jnp
from jax import lax
from jax.experimental import pallas as pl
from jax.experimental.pallas import tpu as pltpu
from jax.sharding import PartitionSpec as P

AXES = ("groups", "lat", "seq")


def place_rows(values, source, filled, leading):
    picked = jnp.where(filled[:, None], values[source], jnp.zeros((), values.dtype))
    return picked.reshape(leading + (values.shape[-1],))


def move_tokens(residual, gradient, block_ids, jump_mask, encoder, enc_bias, decoder, dec_bias):
    tok_rows, width = residual.shape
    active = block_ids.shape[1]
    lanes = jump_mask.shape[2]
    lat_count = lax.axis_size("lat")
    seq_count = lax.axis_size("seq")
    local_blocks = encoder.shape[1] // lanes
    block_count = local_blocks * lat_count
    capacity = max(
        2, min(tok_rows, (3 * tok_rows * active + 2 * block_count - 1) // (2 * block_count))
    )
    slot_count = tok_rows * active
    flat_blocks = block_ids.reshape(slot_count)
    one_hot = (flat_blocks[:, None] == jnp.arange(block_count, dtype=jnp.int32)[None, :]).astype(
        jnp.int32
    )
    earlier = jnp.sum(jnp.cumsum(one_hot, axis=0) * one_hot, axis=1) - 1
    slot_id = flat_blocks * capacity + earlier
    owner_row = (
        jnp.zeros((block_count * capacity,), jnp.int32)
        .at[slot_id]
        .set(jnp.arange(slot_count, dtype=jnp.int32) + 1)
    )
    filled = owner_row > 0
    slot_source = jnp.maximum(owner_row - 1, 0)
    token_source = slot_source // active
    leading = (lat_count, local_blocks, capacity)
    enc_blocks = encoder.reshape(width, local_blocks, lanes)
    dec_blocks = decoder.reshape(local_blocks, lanes, width)
    bias_blocks = enc_bias.reshape(1, local_blocks, 1, lanes)
    mask_values = jump_mask.astype(jnp.float32)
    total_tokens = tok_rows * lat_count * seq_count
    factor = (total_tokens * active / block_count) ** (-0.5)

    def gather_home(slotted):
        last = slotted.shape[-1]
        return slotted.reshape(block_count * capacity, last)[slot_id].reshape(
            tok_rows, active, last
        )

    def swap(values):
        return lax.all_to_all(values, "lat", split_axis=0, concat_axis=0, tiled=True)

    residual_slots = place_rows(residual, token_source, filled, leading)
    gradient_slots = place_rows(gradient, token_source, filled, leading)
    preact = jnp.einsum(
        "sbcd,dbj->sbcj", swap(residual_slots), enc_blocks, preferred_element_type=jnp.float32
    )
    preact = swap((preact + bias_blocks).astype(jnp.bfloat16)).astype(jnp.float32)
    latent_codes = (gather_home(preact) * mask_values).astype(jnp.bfloat16)
    code_slots = place_rows(latent_codes.reshape(slot_count, lanes), slot_source, filled, leading)
    code_data = swap(code_slots)
    grad_data = swap(gradient_slots)
    score_data = code_data.astype(jnp.float32) * jnp.einsum(
        "sbcd,bjd->sbcj", grad_data, dec_blocks, preferred_element_type=jnp.float32
    )
    recon_data = jnp.einsum(
        "sbcj,bjd->sbcd", code_data, dec_blocks, preferred_element_type=jnp.float32
    )
    recon_home = gather_home(swap(recon_data.astype(jnp.bfloat16)))
    attribution = gather_home(swap(score_data))
    recon_error = (
        residual.astype(jnp.float32) - dec_bias - jnp.sum(recon_home.astype(jnp.float32), axis=1)
    ).astype(jnp.bfloat16)
    term = jnp.dot(
        one_hot.T.astype(jnp.float32),
        attribution.reshape(slot_count, lanes),
        precision=lax.Precision.HIGHEST,
    )
    latent_totals = (
        lax.psum_scatter(
            term.reshape(block_count * lanes), ("lat", "seq"), scatter_dimension=0, tiled=True
        )
        * factor
    )
    return (latent_codes, attribution, recon_error, latent_totals)


BF = jnp.bfloat16
F32 = jnp.float32


def nt(a, b):
    return lax.dot_general(a, b, (((1,), (1,)), ((), ())), preferred_element_type=F32)


def along(z):
    return (4 - z) & 3


def place_here():
    lat = lax.axis_index("lat")
    return lax.rem(lat, 2), lax.axis_index("groups"), along(lax.div(lat, 2)), lax.axis_index("seq")


def call(kernel, outs, *args, far=(), scratch=(), vmem=24):
    return pl.pallas_call(
        kernel,
        in_specs=[
            pl.BlockSpec(memory_space=pl.ANY if i in far else pltpu.VMEM) for i in range(len(args))
        ],
        out_specs=[pl.BlockSpec(memory_space=pltpu.VMEM)] * len(outs),
        out_shape=[jax.ShapeDtypeStruct(*o) for o in outs],
        scratch_shapes=list(scratch),
        compiler_params=pltpu.CompilerParams(vmem_limit_bytes=vmem << 20),
    )(*args)


def pick_latents(per, lanes, y):
    row = lax.broadcasted_iota(jnp.int32, (per, lanes), 0)
    lane = lax.broadcasted_iota(jnp.int32, (per, lanes), 1)
    return (lane == row + per * y).astype(BF)


def weights_kernel(enc, dec, bias, out, enc_half, bias_here, sem):
    _, y, _, s = place_here()
    lanes = enc.shape[1]
    half = enc_half.shape[0]
    per = out.shape[0]
    chunks = 4
    n = half // chunks
    side = s * half
    copies = [pltpu.make_async_copy(bias, bias_here, sem.at[2 * chunks])]
    for i in range(chunks):
        copies.append(
            pltpu.make_async_copy(
                enc.at[pl.ds(pl.multiple_of(side + i * n, 64), n), :],
                enc_half.at[pl.ds(i * n, n), :],
                sem.at[i],
            )
        )
    m = per // chunks
    for i in range(chunks):
        copies.append(
            pltpu.make_async_copy(
                dec.at[
                    pl.ds(pl.multiple_of(y * per + i * m, 16), m),
                    pl.ds(pl.multiple_of(side, 128), half),
                ],
                out.at[pl.ds(i * m, m), pl.ds(half + 128, half)],
                sem.at[chunks + i],
            )
        )
    for copy in copies:
        copy.start()
    pick = pick_latents(per, lanes, y)
    copies[0].wait()
    b = bias_here[...]
    hi = b.astype(BF).astype(F32)
    mid = (b - hi).astype(BF).astype(F32)
    low = b - hi - mid
    term = lax.broadcasted_iota(jnp.int32, (lanes, lanes), 0)
    terms = jnp.where(term == 0, hi, jnp.where(term == 1, mid, jnp.where(term == 2, low, 0.0)))
    out[:, half : half + 128] = nt(pick, terms.astype(BF)).astype(BF)
    for copy in copies[1 : chunks + 1]:
        copy.wait()
    out[:, :half] = nt(pick, enc_half[...]).astype(BF)
    for copy in copies[chunks + 1 :]:
        copy.wait()


def totals_kernel(early, two, three, row, rest):
    _, y, _, s = place_here()
    per = row.shape[1]
    total = early[:2] + two[:2] + pltpu.roll(three[...], per, 1)[:2]
    row[...] = jnp.where(y == s, total[:1, :per], total[1:, :per])
    rest[...] = jnp.where(y == s, total[1:, :per], total[:1, :per])


def after_kernel(*refs):
    del refs


def target_block(lane, m, x, z, ring):
    turn = z - 2 * m - (lane >= 64).astype(jnp.int32)
    turn = jnp.where(turn < 0, turn + ring, turn)
    return along(turn) * 2 + x


def tokens_kernel(ring, res, grad, ids, jump, _, to_x, to_y, to_d, own_mask, sem):
    x, y, z, _ = place_here()
    tok, width = res.shape
    active = ids.shape[0]
    outs = (to_x, to_y, to_d)
    copies = []
    for i, src in enumerate((res, grad)):
        for j, out in enumerate(outs):
            copies.append(
                pltpu.make_async_copy(src, out.at[:, pl.ds(i * width, width)], sem.at[3 * i + j])
            )
    for copy in copies:
        copy.start()
    names = ids[...].T
    names = [jnp.broadcast_to(names[:, k : k + 1], (tok, 128)) for k in range(active)]
    lane = lax.broadcasted_iota(jnp.int32, (tok, 128), 1)
    low = lane < 64
    plain = [jump[:, k, :] for k in range(active)]
    moved = [pltpu.roll(v, 64, 1) for v in plain]
    for dest in range(4):
        x_rel, y_rel = dest % 2, dest // 2
        first = (y ^ y_rel) == 0
        for m in range(ring // 2):
            tgt = target_block(lane, m, x ^ x_rel, z, ring)
            total = jnp.zeros((tok, 128), jnp.int32)
            for k in range(active):
                value = jnp.where(low == first, plain[k], moved[k])
                total = total + jnp.where(names[k] == tgt, value, 0)
            out = total.astype(F32).astype(BF)
            if dest == 0:
                own_mask[:, m * 128 : m * 128 + 128] = out
            else:
                at = 2 * width + m * 128
                outs[dest - 1][:, at : at + 128] = out
    for copy in copies:
        copy.wait()


def group_sums(scores):
    half = scores.shape[0] // 2
    near = jnp.sum(scores[:half], axis=0, keepdims=True)
    far = jnp.sum(scores[half:], axis=0, keepdims=True)
    return jnp.concatenate([near, far, jnp.zeros((6, scores.shape[1]), F32)], axis=0)


def blocks(rows, mask, sides, half):
    bias = jnp.concatenate([p[:, half : half + 128] for p in sides[0]], axis=0)
    preact = nt(jnp.ones((8, 128), BF), bias)[:1]
    for j, parts in enumerate(sides):
        weights = jnp.concatenate([p[:, :half] for p in parts], axis=0)
        preact = preact + nt(rows[:, j * half : (j + 1) * half], weights)
    code = (preact * mask.astype(F32)).astype(BF)
    proj = jnp.zeros(code.shape, F32)
    recon = []
    for j, parts in enumerate(sides):
        weights = jnp.concatenate([p[:, half + 128 :] for p in parts], axis=0)
        proj = proj + nt(rows[:, (2 + j) * half : (3 + j) * half], weights)
        recon.append(jnp.dot(code, weights, preferred_element_type=F32))
    return code, code.astype(F32) * proj, recon


def early_kernel(
    from_d, from_x, from_y, own, own_mask, enc, dec, mine_0, mine_1, other_1,
    rows, mask, recon, codes, scores, sums, enc_half, other_0, sem,
):
    _, y, _, s = place_here()
    tok = own.shape[0]
    per, lanes = other_0.shape[0], enc.shape[1]
    half = enc_half.shape[0]
    width = 2 * half
    far = pl.ds(pl.multiple_of((1 - s) * half, 128), half)
    get_enc = pltpu.make_async_copy(enc.at[far, :], enc_half, sem.at[0])
    get_dec = pltpu.make_async_copy(
        dec.at[pl.ds(pl.multiple_of(y * per, 16), per), far],
        other_0.at[:, pl.ds(half + 128, half)],
        sem.at[1],
    )
    get_enc.start()
    get_dec.start()
    for i, src in enumerate((own, from_x, from_y, from_d)):
        at = slice(i * tok, (i + 1) * tok)
        mask[at] = own_mask[...] if i == 0 else src[:, 2 * width :]
        for j in range(4):
            side = s if j % 2 == 0 else 1 - s
            cols = pl.ds(pl.multiple_of(width * (j // 2) + side * half, 128), half)
            rows[at, j * half : (j + 1) * half] = src[:, cols]
    other_0[:, half : half + 128] = jnp.zeros((per, 128), BF)
    get_enc.wait()
    other_0[:, :half] = nt(pick_latents(per, lanes, y), enc_half[...]).astype(BF)
    get_dec.wait()
    code, score, total = blocks(
        rows, mask[:, : 2 * per], ((mine_0, mine_1), (other_0, other_1)), half
    )
    codes[...] = code
    scores[...] = score
    for j in range(2):
        recon[:, j * half : (j + 1) * half] = total[j]
    sums[...] = group_sums(score)


def late_kernel(
    rows, mask, recon, codes, scores, mine_2, other_2, mine_3, other_3, sums, one,
    own_recon, own_codes, own_scores, to_x, to_y, to_d, sums_23, sums_01,
):
    _, _, _, s = place_here()
    per = mine_2.shape[0]
    tok = own_codes.shape[0]
    width = own_recon.shape[1]
    half = width // 2
    code, score, total = blocks(
        rows, mask[:, 2 * per :], ((mine_2, mine_3), (other_2, other_3)), half
    )
    for j in range(2):
        cols = pl.ds(pl.multiple_of((s if j == 0 else 1 - s) * half, 128), half)
        part = recon[:, j * half : (j + 1) * half] + total[j]
        for i, out in enumerate((own_recon, to_x, to_y, to_d)):
            out[:, cols] = part[i * tok : (i + 1) * tok].astype(out.dtype)
    sums_23[...] = group_sums(score)
    sums_01[...] = sums[...] + pltpu.roll(one[...], per, 1)
    own_codes[...] = jnp.concatenate([codes[:tok], code[:tok]], axis=1)
    own_scores[...] = jnp.concatenate([scores[:tok], score[:tok]], axis=1)
    for i, out in enumerate((to_x, to_y, to_d)):
        at = slice((i + 1) * tok, (i + 2) * tok)
        for j, (first, second) in enumerate(((codes, code), (scores, score))):
            base = width + 4 * per * j
            out[:, base : base + 2 * per] = first[at].astype(BF)
            out[:, base + 2 * per : base + 4 * per] = second[at].astype(BF)


def final_kernel(
    ring, factor, from_d, from_x, from_y, own_recon, own_codes, own_scores, own, dec_bias, ids, row, rest,
    out_codes, out_scores, out_error, out_totals,
):
    x, y, z, _ = place_here()
    out_totals[...] = (row[...] + rest[...]) * factor
    tok, width = own_recon.shape
    names = own_codes.shape[1]
    active = ids.shape[0]
    named = ids[...].T
    named = [jnp.broadcast_to(named[:, k : k + 1], (tok, 128)) for k in range(active)]
    others = (from_x, from_y, from_d)
    recon = own_recon[...]
    for src in others:
        recon = recon + src[:, :width].astype(F32)
    out_error[...] = (own[:, :width].astype(F32) - dec_bias[...] - recon).astype(BF)
    code_src = [own_codes[...].astype(F32)]
    score_src = [own_scores[...]]
    for src in others:
        code_src.append(src[:, width : width + names].astype(F32))
        score_src.append(src[:, width + names :].astype(F32))
    lane = lax.broadcasted_iota(jnp.int32, (tok, 128), 1)
    low = lane < 64
    code_out = [jnp.zeros((tok, 128), F32)] * active
    score_out = [jnp.zeros((tok, 128), F32)] * active
    for x_rel in range(2):
        for kk in range(ring):
            cols = slice(128 * (kk // 2), 128 * (kk // 2) + 128)
            turn = z - kk
            turn = jnp.where(turn < 0, turn + ring, turn)
            block = along(turn) * 2 + (x ^ x_rel)
            pair = []
            for src in (code_src, score_src):
                near, far = src[x_rel][:, cols], src[2 + x_rel][:, cols]
                first = jnp.where(y == 0, near, far)
                second = jnp.where(y == 0, far, near)
                if kk % 2 == 0:
                    pair.append(jnp.where(low, first, pltpu.roll(second, 64, 1)))
                else:
                    pair.append(jnp.where(low, pltpu.roll(first, 64, 1), second))
            for k in range(active):
                hit = named[k] == block
                code_out[k] = code_out[k] + jnp.where(hit, pair[0], 0.0)
                score_out[k] = score_out[k] + jnp.where(hit, pair[1], 0.0)
    for k in range(active):
        out_codes[:, k, :] = code_out[k].astype(BF)
        out_scores[:, k, :] = score_out[k]


def move_weights(residual, gradient, block_ids, jump_mask, encoder, enc_bias, decoder, dec_bias):
    tok, width = residual.shape
    active = block_ids.shape[1]
    lanes = jump_mask.shape[2]
    lat_count = lax.axis_size("lat")
    ring = lat_count // 2
    per = lanes // 2
    half = width // 2
    names = ring * per

    def permute(values, to):
        pairs = []
        for gg in range(2):
            for ll in range(lat_count):
                for ss in range(2):
                    a, b, c = to(gg, ll, ss)
                    pairs.append(((gg * lat_count + ll) * 2 + ss, (a * lat_count + b) * 2 + c))
        return lax.ppermute(values, AXES, pairs)

    def by_x(v):
        return permute(v, lambda gg, ll, ss: (gg, ll ^ 1, ss))

    def by_y(v):
        return permute(v, lambda gg, ll, ss: (1 - gg, ll, ss))

    def by_xy(v):
        return permute(v, lambda gg, ll, ss: (1 - gg, ll ^ 1, ss))

    def by_core(v):
        return permute(v, lambda gg, ll, ss: (gg, ll, 1 - ss))

    def by_z(v, k):
        return permute(
            v, lambda gg, ll, ss: (gg, 2 * along((along(ll // 2) + k) % ring) + ll % 2, ss)
        )

    (own,) = call(
        weights_kernel,
        [((per, 2 * half + 128), BF)],
        encoder, decoder, enc_bias.reshape(1, lanes),
        far=(0, 1, 2),
        scratch=[
            pltpu.VMEM((half, lanes), BF),
            pltpu.VMEM((1, lanes), F32),
            pltpu.SemaphoreType.DMA((9,)),
        ],
        vmem=56,
    )
    part_1 = by_z(own, 1)
    part_2 = by_z(part_1, 1)
    part_3 = by_z(own, -1)

    to_x, to_y, to_d, own_mask = call(
        functools.partial(tokens_kernel, ring),
        [((tok, 2 * width + names), BF)] * 3 + [((tok, names), BF)],
        residual, gradient, block_ids.T, jump_mask, own,
        far=(0, 1, 4),
        scratch=[pltpu.SemaphoreType.DMA((6,))],
    )
    own_rows = to_d
    from_d = by_xy(to_d)
    from_x = by_x(to_x)
    from_y = by_y(to_y)
    rows, mask, recon, codes, scores, sums = call(
        early_kernel,
        [
            ((4 * tok, 2 * width), BF),
            ((4 * tok, names), BF),
            ((4 * tok, width), F32),
            ((4 * tok, 2 * per), BF),
            ((4 * tok, 2 * per), F32),
            ((8, 2 * per), F32),
        ],
        from_d, from_x, from_y, own_rows, own_mask, encoder, decoder,
        own, part_1, by_core(part_1),
        far=(5, 6),
        scratch=[
            pltpu.VMEM((half, lanes), BF),
            pltpu.VMEM((per, 2 * half + 128), BF),
            pltpu.SemaphoreType.DMA((2,)),
        ],
    )
    part_2 = pl.pallas_call(
        after_kernel,
        in_specs=[pl.BlockSpec(memory_space=pl.ANY)] * 2,
        out_specs=pl.BlockSpec(memory_space=pl.ANY),
        out_shape=jax.ShapeDtypeStruct(part_2.shape, BF),
        input_output_aliases={0: 0},
        compiler_params=pltpu.CompilerParams(vmem_limit_bytes=1 << 20),
    )(part_2, codes)
    own_recon, own_codes, own_scores, to_x, to_y, to_d, sums_23, sums_01 = call(
        late_kernel,
        [((tok, width), F32), ((tok, names), BF), ((tok, names), F32)]
        + [((tok, width + 2 * names), BF)] * 3
        + [((8, 2 * per), F32)] * 2,
        rows, mask, recon, codes, scores, part_2, by_core(part_2), part_3, by_core(part_3),
        sums, by_z(sums, -1),
    )
    from_d = by_xy(to_d)
    from_x = by_x(to_x)
    from_y = by_y(to_y)

    row, rest = call(
        totals_kernel,
        [((1, per), F32)] * 2,
        sums_01, by_z(sums_23, -2), by_z(sums_23, 1),
    )
    factor = (tok * lat_count * 2 * active / lat_count) ** (-0.5)
    latent_codes, attribution, recon_error, latent_totals = call(
        functools.partial(final_kernel, ring, factor),
        [
            ((tok, active, lanes), BF),
            ((tok, active, lanes), F32),
            ((tok, width), BF),
            ((1, per), F32),
        ],
        from_d, from_x, from_y, own_recon, own_codes, own_scores,
        own_rows, dec_bias.reshape(1, width), block_ids.T,
        permute(row, lambda gg, ll, ss: (ss, ll, gg)),
        permute(rest, lambda gg, ll, ss: (1 - ss, ll, gg)),
    )
    return (latent_codes, attribution, recon_error, latent_totals.reshape(per))


def solution(mesh):
    sizes = dict(mesh.shape)

    def on_device(residual, gradient, block_ids, jump_mask, encoder, enc_bias, decoder, dec_bias):
        lanes = jump_mask.shape[2]
        small = (
            sizes["groups"] == 2
            and sizes["seq"] == 2
            and sizes["lat"] == 8
            and encoder.shape[1] == lanes
            and lanes == 128
            and residual.shape[0] % 16 == 0
            and residual.shape[1] % 256 == 0
        )
        body = move_weights if small else move_tokens
        return body(
            residual, gradient, block_ids, jump_mask, encoder, enc_bias, decoder, dec_bias
        )

    rows = P(("groups", "lat", "seq"), None)
    cubes = P(("groups", "lat", "seq"), None, None)
    return jax.shard_map(
        on_device,
        mesh=mesh,
        in_specs=(rows, rows, rows, cubes, P(None, "lat"), P("lat"), P("lat", None), P()),
        out_specs=(cubes, cubes, rows, P(("groups", "lat", "seq"))),
        check_vma=False,
    )
```

```python
import functools

import jax
import jax.numpy as jnp
from jax import lax
from jax.experimental import pallas as pl
from jax.experimental.pallas import tpu as pltpu
from jax.sharding import PartitionSpec as P

AXES = ("groups", "lat", "seq")


def place_rows(values, source, filled, leading):
    picked = jnp.where(filled[:, None], values[source], jnp.zeros((), values.dtype))
    return picked.reshape(leading + (values.shape[-1],))


def move_tokens(residual, gradient, block_ids, jump_mask, encoder, enc_bias, decoder, dec_bias):
    tok_rows, width = residual.shape
    active = block_ids.shape[1]
    lanes = jump_mask.shape[2]
    lat_count = lax.axis_size("lat")
    seq_count = lax.axis_size("seq")
    local_blocks = encoder.shape[1] // lanes
    block_count = local_blocks * lat_count
    capacity = max(
        2, min(tok_rows, (3 * tok_rows * active + 2 * block_count - 1) // (2 * block_count))
    )
    slot_count = tok_rows * active
    flat_blocks = block_ids.reshape(slot_count)
    one_hot = (flat_blocks[:, None] == jnp.arange(block_count, dtype=jnp.int32)[None, :]).astype(
        jnp.int32
    )
    earlier = jnp.sum(jnp.cumsum(one_hot, axis=0) * one_hot, axis=1) - 1
    slot_id = flat_blocks * capacity + earlier
    owner_row = (
        jnp.zeros((block_count * capacity,), jnp.int32)
        .at[slot_id]
        .set(jnp.arange(slot_count, dtype=jnp.int32) + 1)
    )
    filled = owner_row > 0
    slot_source = jnp.maximum(owner_row - 1, 0)
    token_source = slot_source // active
    leading = (lat_count, local_blocks, capacity)
    enc_blocks = encoder.reshape(width, local_blocks, lanes)
    dec_blocks = decoder.reshape(local_blocks, lanes, width)
    bias_blocks = enc_bias.reshape(1, local_blocks, 1, lanes)
    mask_values = jump_mask.astype(jnp.float32)
    total_tokens = tok_rows * lat_count * seq_count
    factor = (total_tokens * active / block_count) ** (-0.5)

    def gather_home(slotted):
        last = slotted.shape[-1]
        return slotted.reshape(block_count * capacity, last)[slot_id].reshape(
            tok_rows, active, last
        )

    def swap(values):
        return lax.all_to_all(values, "lat", split_axis=0, concat_axis=0, tiled=True)

    residual_slots = place_rows(residual, token_source, filled, leading)
    gradient_slots = place_rows(gradient, token_source, filled, leading)
    preact = jnp.einsum(
        "sbcd,dbj->sbcj", swap(residual_slots), enc_blocks, preferred_element_type=jnp.float32
    )
    preact = swap((preact + bias_blocks).astype(jnp.bfloat16)).astype(jnp.float32)
    latent_codes = (gather_home(preact) * mask_values).astype(jnp.bfloat16)
    code_slots = place_rows(latent_codes.reshape(slot_count, lanes), slot_source, filled, leading)
    code_data = swap(code_slots)
    grad_data = swap(gradient_slots)
    score_data = code_data.astype(jnp.float32) * jnp.einsum(
        "sbcd,bjd->sbcj", grad_data, dec_blocks, preferred_element_type=jnp.float32
    )
    recon_data = jnp.einsum(
        "sbcj,bjd->sbcd", code_data, dec_blocks, preferred_element_type=jnp.float32
    )
    recon_home = gather_home(swap(recon_data.astype(jnp.bfloat16)))
    attribution = gather_home(swap(score_data))
    recon_error = (
        residual.astype(jnp.float32) - dec_bias - jnp.sum(recon_home.astype(jnp.float32), axis=1)
    ).astype(jnp.bfloat16)
    term = jnp.dot(
        one_hot.T.astype(jnp.float32),
        attribution.reshape(slot_count, lanes),
        precision=lax.Precision.HIGHEST,
    )
    latent_totals = (
        lax.psum_scatter(
            term.reshape(block_count * lanes), ("lat", "seq"), scatter_dimension=0, tiled=True
        )
        * factor
    )
    return (latent_codes, attribution, recon_error, latent_totals)


BF = jnp.bfloat16
F32 = jnp.float32


def nt(a, b):
    return lax.dot_general(a, b, (((1,), (1,)), ((), ())), preferred_element_type=F32)


def along(z):
    return (4 - z) & 3


def place_here():
    lat = lax.axis_index("lat")
    return lax.rem(lat, 2), lax.axis_index("groups"), along(lax.div(lat, 2)), lax.axis_index("seq")


def call(kernel, outs, *args, far=(), scratch=(), vmem=24):
    return pl.pallas_call(
        kernel,
        in_specs=[
            pl.BlockSpec(memory_space=pl.ANY if i in far else pltpu.VMEM) for i in range(len(args))
        ],
        out_specs=[pl.BlockSpec(memory_space=pltpu.VMEM)] * len(outs),
        out_shape=[jax.ShapeDtypeStruct(*o) for o in outs],
        scratch_shapes=list(scratch),
        compiler_params=pltpu.CompilerParams(vmem_limit_bytes=vmem << 20),
    )(*args)


def pick_latents(per, lanes, y):
    row = lax.broadcasted_iota(jnp.int32, (per, lanes), 0)
    lane = lax.broadcasted_iota(jnp.int32, (per, lanes), 1)
    return (lane == row + per * y).astype(BF)


def weights_kernel(enc, dec, bias, out, enc_half, bias_here, sem):
    _, y, _, s = place_here()
    lanes = enc.shape[1]
    half = enc_half.shape[0]
    per = out.shape[0]
    chunks = 4
    n = half // chunks
    side = s * half
    copies = [pltpu.make_async_copy(bias, bias_here, sem.at[2 * chunks])]
    for i in range(chunks):
        copies.append(
            pltpu.make_async_copy(
                enc.at[pl.ds(pl.multiple_of(side + i * n, 64), n), :],
                enc_half.at[pl.ds(i * n, n), :],
                sem.at[i],
            )
        )
    m = per // chunks
    for i in range(chunks):
        copies.append(
            pltpu.make_async_copy(
                dec.at[
                    pl.ds(pl.multiple_of(y * per + i * m, 16), m),
                    pl.ds(pl.multiple_of(side, 128), half),
                ],
                out.at[pl.ds(i * m, m), pl.ds(half + 128, half)],
                sem.at[chunks + i],
            )
        )
    for copy in copies:
        copy.start()
    pick = pick_latents(per, lanes, y)
    copies[0].wait()
    b = bias_here[...]
    hi = b.astype(BF).astype(F32)
    mid = (b - hi).astype(BF).astype(F32)
    low = b - hi - mid
    term = lax.broadcasted_iota(jnp.int32, (lanes, lanes), 0)
    terms = jnp.where(term == 0, hi, jnp.where(term == 1, mid, jnp.where(term == 2, low, 0.0)))
    out[:, half : half + 128] = nt(pick, terms.astype(BF)).astype(BF)
    for copy in copies[1 : chunks + 1]:
        copy.wait()
    out[:, :half] = nt(pick, enc_half[...]).astype(BF)
    for copy in copies[chunks + 1 :]:
        copy.wait()


def totals_kernel(early, one, two, three, row, rest):
    _, y, _, s = place_here()
    per = row.shape[1]
    total = early[:2] + two[:2] + pltpu.roll(one[...] + three[...], per, 1)[:2]
    row[...] = jnp.where(y == s, total[:1, :per], total[1:, :per])
    rest[...] = jnp.where(y == s, total[1:, :per], total[:1, :per])


def after_kernel(*refs):
    del refs


def target_block(lane, m, x, z, ring):
    turn = z - 2 * m - (lane >= 64).astype(jnp.int32)
    turn = jnp.where(turn < 0, turn + ring, turn)
    return along(turn) * 2 + x


def tokens_kernel(ring, res, grad, ids, jump, _, to_x, to_y, to_d, own_mask, sem):
    x, y, z, _ = place_here()
    tok, width = res.shape
    active = ids.shape[0]
    outs = (to_x, to_y, to_d)
    copies = []
    for i, src in enumerate((res, grad)):
        for j, out in enumerate(outs):
            copies.append(
                pltpu.make_async_copy(src, out.at[:, pl.ds(i * width, width)], sem.at[3 * i + j])
            )
    for copy in copies:
        copy.start()
    names = ids[...].T
    names = [jnp.broadcast_to(names[:, k : k + 1], (tok, 128)) for k in range(active)]
    lane = lax.broadcasted_iota(jnp.int32, (tok, 128), 1)
    low = lane < 64
    plain = [jump[:, k, :] for k in range(active)]
    moved = [pltpu.roll(v, 64, 1) for v in plain]
    for dest in range(4):
        x_rel, y_rel = dest % 2, dest // 2
        first = (y ^ y_rel) == 0
        for m in range(ring // 2):
            tgt = target_block(lane, m, x ^ x_rel, z, ring)
            total = jnp.zeros((tok, 128), jnp.int32)
            for k in range(active):
                value = jnp.where(low == first, plain[k], moved[k])
                total = total + jnp.where(names[k] == tgt, value, 0)
            out = total.astype(F32).astype(BF)
            if dest == 0:
                own_mask[:, m * 128 : m * 128 + 128] = out
            else:
                at = 2 * width + m * 128
                outs[dest - 1][:, at : at + 128] = out
    for copy in copies:
        copy.wait()


def group_sums(scores):
    half = scores.shape[0] // 2
    near = jnp.sum(scores[:half], axis=0, keepdims=True)
    far = jnp.sum(scores[half:], axis=0, keepdims=True)
    return jnp.concatenate([near, far, jnp.zeros((6, scores.shape[1]), F32)], axis=0)


def blocks(rows, mask, sides, half):
    bias = jnp.concatenate([p[:, half : half + 128] for p in sides[0]], axis=0)
    preact = nt(jnp.ones((8, 128), BF), bias)[:1]
    for j, parts in enumerate(sides):
        weights = jnp.concatenate([p[:, :half] for p in parts], axis=0)
        preact = preact + nt(rows[:, j * half : (j + 1) * half], weights)
    code = (preact * mask.astype(F32)).astype(BF)
    proj = jnp.zeros(code.shape, F32)
    recon = []
    for j, parts in enumerate(sides):
        weights = jnp.concatenate([p[:, half + 128 :] for p in parts], axis=0)
        proj = proj + nt(rows[:, (2 + j) * half : (3 + j) * half], weights)
        recon.append(jnp.dot(code, weights, preferred_element_type=F32))
    return code, code.astype(F32) * proj, recon


def early_kernel(
    from_d, from_x, from_y, own, own_mask, enc, dec, mine_0, mine_1, other_1,
    rows, mask, recon, codes, scores, sums, enc_half, other_0, sem,
):
    _, y, _, s = place_here()
    tok = own.shape[0]
    per, lanes = other_0.shape[0], enc.shape[1]
    half = enc_half.shape[0]
    width = 2 * half
    far = pl.ds(pl.multiple_of((1 - s) * half, 128), half)
    get_enc = pltpu.make_async_copy(enc.at[far, :], enc_half, sem.at[0])
    get_dec = pltpu.make_async_copy(
        dec.at[pl.ds(pl.multiple_of(y * per, 16), per), far],
        other_0.at[:, pl.ds(half + 128, half)],
        sem.at[1],
    )
    get_enc.start()
    get_dec.start()
    for i, src in enumerate((own, from_x, from_y, from_d)):
        at = slice(i * tok, (i + 1) * tok)
        mask[at] = own_mask[...] if i == 0 else src[:, 2 * width :]
        for j in range(4):
            side = s if j % 2 == 0 else 1 - s
            cols = pl.ds(pl.multiple_of(width * (j // 2) + side * half, 128), half)
            rows[at, j * half : (j + 1) * half] = src[:, cols]
    other_0[:, half : half + 128] = jnp.zeros((per, 128), BF)
    get_enc.wait()
    other_0[:, :half] = nt(pick_latents(per, lanes, y), enc_half[...]).astype(BF)
    get_dec.wait()
    code, score, total = blocks(
        rows, mask[:, : 2 * per], ((mine_0, mine_1), (other_0, other_1)), half
    )
    codes[...] = code
    scores[...] = score
    for j in range(2):
        recon[:, j * half : (j + 1) * half] = total[j]
    sums[...] = group_sums(score)


def late_kernel(
    rows, mask, recon, codes, scores, mine_2, other_2, mine_3, other_3,
    own_recon, own_codes, own_scores, to_x, to_y, to_d, sums_23,
):
    _, _, _, s = place_here()
    per = mine_2.shape[0]
    tok = own_codes.shape[0]
    width = own_recon.shape[1]
    half = width // 2
    code, score, total = blocks(
        rows, mask[:, 2 * per :], ((mine_2, mine_3), (other_2, other_3)), half
    )
    for j in range(2):
        cols = pl.ds(pl.multiple_of((s if j == 0 else 1 - s) * half, 128), half)
        part = recon[:, j * half : (j + 1) * half] + total[j]
        for i, out in enumerate((own_recon, to_x, to_y, to_d)):
            out[:, cols] = part[i * tok : (i + 1) * tok].astype(out.dtype)
    sums_23[...] = group_sums(score)
    own_codes[...] = jnp.concatenate([codes[:tok], code[:tok]], axis=1)
    own_scores[...] = jnp.concatenate([scores[:tok], score[:tok]], axis=1)
    for i, out in enumerate((to_x, to_y, to_d)):
        at = slice((i + 1) * tok, (i + 2) * tok)
        for j, (first, second) in enumerate(((codes, code), (scores, score))):
            base = width + 4 * per * j
            out[:, base : base + 2 * per] = first[at].astype(BF)
            out[:, base + 2 * per : base + 4 * per] = second[at].astype(BF)


def final_kernel(
    ring, factor, from_d, from_x, from_y, own_recon, own_codes, own_scores, own, dec_bias, ids, row, rest,
    out_codes, out_scores, out_error, out_totals,
):
    x, y, z, _ = place_here()
    out_totals[...] = (row[...] + rest[...]) * factor
    tok, width = own_recon.shape
    names = own_codes.shape[1]
    active = ids.shape[0]
    named = ids[...].T
    named = [jnp.broadcast_to(named[:, k : k + 1], (tok, 128)) for k in range(active)]
    others = (from_x, from_y, from_d)
    recon = own_recon[...]
    for src in others:
        recon = recon + src[:, :width].astype(F32)
    out_error[...] = (own[:, :width].astype(F32) - dec_bias[...] - recon).astype(BF)
    code_src = [own_codes[...].astype(F32)]
    score_src = [own_scores[...]]
    for src in others:
        code_src.append(src[:, width : width + names].astype(F32))
        score_src.append(src[:, width + names :].astype(F32))
    lane = lax.broadcasted_iota(jnp.int32, (tok, 128), 1)
    low = lane < 64
    code_out = [jnp.zeros((tok, 128), F32)] * active
    score_out = [jnp.zeros((tok, 128), F32)] * active
    for x_rel in range(2):
        for kk in range(ring):
            cols = slice(128 * (kk // 2), 128 * (kk // 2) + 128)
            turn = z - kk
            turn = jnp.where(turn < 0, turn + ring, turn)
            block = along(turn) * 2 + (x ^ x_rel)
            pair = []
            for src in (code_src, score_src):
                near, far = src[x_rel][:, cols], src[2 + x_rel][:, cols]
                first = jnp.where(y == 0, near, far)
                second = jnp.where(y == 0, far, near)
                if kk % 2 == 0:
                    pair.append(jnp.where(low, first, pltpu.roll(second, 64, 1)))
                else:
                    pair.append(jnp.where(low, pltpu.roll(first, 64, 1), second))
            for k in range(active):
                hit = named[k] == block
                code_out[k] = code_out[k] + jnp.where(hit, pair[0], 0.0)
                score_out[k] = score_out[k] + jnp.where(hit, pair[1], 0.0)
    for k in range(active):
        out_codes[:, k, :] = code_out[k].astype(BF)
        out_scores[:, k, :] = score_out[k]


def move_weights(residual, gradient, block_ids, jump_mask, encoder, enc_bias, decoder, dec_bias):
    tok, width = residual.shape
    active = block_ids.shape[1]
    lanes = jump_mask.shape[2]
    lat_count = lax.axis_size("lat")
    ring = lat_count // 2
    per = lanes // 2
    half = width // 2
    names = ring * per

    def permute(values, to):
        pairs = []
        for gg in range(2):
            for ll in range(lat_count):
                for ss in range(2):
                    a, b, c = to(gg, ll, ss)
                    pairs.append(((gg * lat_count + ll) * 2 + ss, (a * lat_count + b) * 2 + c))
        return lax.ppermute(values, AXES, pairs)

    def by_x(v):
        return permute(v, lambda gg, ll, ss: (gg, ll ^ 1, ss))

    def by_y(v):
        return permute(v, lambda gg, ll, ss: (1 - gg, ll, ss))

    def by_xy(v):
        return permute(v, lambda gg, ll, ss: (1 - gg, ll ^ 1, ss))

    def by_core(v):
        return permute(v, lambda gg, ll, ss: (gg, ll, 1 - ss))

    def by_z(v, k):
        return permute(
            v, lambda gg, ll, ss: (gg, 2 * along((along(ll // 2) + k) % ring) + ll % 2, ss)
        )

    (own,) = call(
        weights_kernel,
        [((per, 2 * half + 128), BF)],
        encoder, decoder, enc_bias.reshape(1, lanes),
        far=(0, 1, 2),
        scratch=[
            pltpu.VMEM((half, lanes), BF),
            pltpu.VMEM((1, lanes), F32),
            pltpu.SemaphoreType.DMA((9,)),
        ],
        vmem=56,
    )
    part_1 = by_z(own, 1)
    part_2 = by_z(part_1, 1)
    part_3 = by_z(own, -1)

    to_x, to_y, to_d, own_mask = call(
        functools.partial(tokens_kernel, ring),
        [((tok, 2 * width + names), BF)] * 3 + [((tok, names), BF)],
        residual, gradient, block_ids.T, jump_mask, own,
        far=(0, 1, 4),
        scratch=[pltpu.SemaphoreType.DMA((6,))],
    )
    own_rows = to_d
    from_d = by_xy(to_d)
    from_x = by_x(to_x)
    from_y = by_y(to_y)
    rows, mask, recon, codes, scores, sums = call(
        early_kernel,
        [
            ((4 * tok, 2 * width), BF),
            ((4 * tok, names), BF),
            ((4 * tok, width), F32),
            ((4 * tok, 2 * per), BF),
            ((4 * tok, 2 * per), F32),
            ((8, 2 * per), F32),
        ],
        from_d, from_x, from_y, own_rows, own_mask, encoder, decoder,
        own, part_1, by_core(part_1),
        far=(5, 6),
        scratch=[
            pltpu.VMEM((half, lanes), BF),
            pltpu.VMEM((per, 2 * half + 128), BF),
            pltpu.SemaphoreType.DMA((2,)),
        ],
    )
    part_2 = pl.pallas_call(
        after_kernel,
        in_specs=[pl.BlockSpec(memory_space=pl.ANY)] * 2,
        out_specs=pl.BlockSpec(memory_space=pl.ANY),
        out_shape=jax.ShapeDtypeStruct(part_2.shape, BF),
        input_output_aliases={0: 0},
        compiler_params=pltpu.CompilerParams(vmem_limit_bytes=1 << 20),
    )(part_2, codes)
    own_recon, own_codes, own_scores, to_x, to_y, to_d, sums_23 = call(
        late_kernel,
        [((tok, width), F32), ((tok, names), BF), ((tok, names), F32)]
        + [((tok, width + 2 * names), BF)] * 3
        + [((8, 2 * per), F32)],
        rows, mask, recon, codes, scores, part_2, by_core(part_2), part_3, by_core(part_3),
    )
    from_d = by_xy(to_d)
    from_x = by_x(to_x)
    from_y = by_y(to_y)

    row, rest = call(
        totals_kernel,
        [((1, per), F32)] * 2,
        sums, by_z(sums, -1), by_z(sums_23, -2), by_z(sums_23, 1),
    )
    factor = (tok * lat_count * 2 * active / lat_count) ** (-0.5)
    latent_codes, attribution, recon_error, latent_totals = call(
        functools.partial(final_kernel, ring, factor),
        [
            ((tok, active, lanes), BF),
            ((tok, active, lanes), F32),
            ((tok, width), BF),
            ((1, per), F32),
        ],
        from_d, from_x, from_y, own_recon, own_codes, own_scores,
        own_rows, dec_bias.reshape(1, width), block_ids.T,
        permute(row, lambda gg, ll, ss: (ss, ll, gg)),
        permute(rest, lambda gg, ll, ss: (1 - ss, ll, gg)),
    )
    return (latent_codes, attribution, recon_error, latent_totals.reshape(per))


def solution(mesh):
    sizes = dict(mesh.shape)

    def on_device(residual, gradient, block_ids, jump_mask, encoder, enc_bias, decoder, dec_bias):
        lanes = jump_mask.shape[2]
        small = (
            sizes["groups"] == 2
            and sizes["seq"] == 2
            and sizes["lat"] == 8
            and encoder.shape[1] == lanes
            and lanes == 128
            and residual.shape[0] % 16 == 0
            and residual.shape[1] % 256 == 0
        )
        body = move_weights if small else move_tokens
        return body(
            residual, gradient, block_ids, jump_mask, encoder, enc_bias, decoder, dec_bias
        )

    rows = P(("groups", "lat", "seq"), None)
    cubes = P(("groups", "lat", "seq"), None, None)
    return jax.shard_map(
        on_device,
        mesh=mesh,
        in_specs=(rows, rows, rows, cubes, P(None, "lat"), P("lat"), P("lat", None), P()),
        out_specs=(cubes, cubes, rows, P(("groups", "lat", "seq"))),
        check_vma=False,
    )
```
